512 devices in a mesh: row: 16 (over x, y_hi, core), col: 32 (over z, y_lo).
Axes of the slice: x: 4, y: 4 (y_hi: 2, y_lo: 2; y = y_hi * 2 + y_lo), z: 16, core: 2. Of those that a mesh axis runs over, the one named last changes fastest.
Arguments:
- hologram: float32 [2, 512, 32768], P(None, 'row', 'col'), may hold values from -24 to 24
- target: bfloat16 [16, 1024, 4096], P('row', 'col'), may hold values from 0.019897461 to 2
Outputs:
- gradient: float32 [2, 512, 32768], P(None, 'row', 'col')
The draws below stay inside these ranges and needn't reach their ends.
All inputs are finite; a program needn't handle non-finite values.
Results may differ from the reference program's by a relative error of at most 0.0003.
Values sent between devices are 32-bit elements; how exact they have to be, the bound alone decides.
No kernel may reach another device: no remote copies, remote signals or barrier semaphores. Data moves between devices by JAX's collectives and lax.ppermute only.
A program may use at most 64 MiB of HBM per device.

```python
import math
import jax
import jax.numpy as jnp
from jax import lax

WIN = 64
NR = 512
NC = 32768
NWR = 16
NWC = 1024


def draw_hologram(key, part):
    key = jax.random.fold_in(key, 7)
    keys = jax.random.split(key, 3)
    row_pos = (jnp.arange(NR, dtype=jnp.float32) + 0.5) / NR - 0.5
    col_pos = (jnp.arange(NC, dtype=jnp.float32) + 0.5) / NC - 0.5
    base = jax.random.truncated_normal(keys[0], -4.0, 4.0, (2, NR, NC), jnp.float32)
    spread = math.log(10.0) / 4
    trend = math.log(3.0) / 2
    row_log = jax.random.uniform(keys[1], (NR,), jnp.float32, -spread, spread) + trend * row_pos
    col_log = jax.random.uniform(keys[2], (NC,), jnp.float32, -spread, spread) + trend * col_pos
    return base * jnp.exp(row_log)[:, None] * jnp.exp(col_log)[None, :]


def block_levels(rng, dims, cuts, smallest, largest):
    gain, own = 1.0, jax.random.fold_in(rng, 6)
    for dim, shards_of in cuts:
        draws = jnp.exp(jax.random.uniform(jax.random.fold_in(own, dim), (shards_of,), jnp.float32, smallest / len(cuts), largest / len(cuts)))
        gain = gain * jnp.repeat(draws, dims[dim] // shards_of).reshape([-1 if axis == dim else 1 for axis in range(len(dims))])
    return gain


def setup_inputs(seed: int = 0) -> dict:
    arg_keys = jax.random.split(jax.random.key(seed), 3)
    return {
        "hologram": draw_hologram(jax.random.fold_in(arg_keys[2], 71), 0),
        "target": jnp.clip(jnp.exp(math.log(2.0) - 4.61031033 * jax.random.uniform(arg_keys[1], (NWR, NWC, WIN * WIN), jnp.float32) ** block_levels(arg_keys[1], (NWR, NWC, WIN * WIN), ((0, 16), (1, 32)), -0.2, 0.2)), 0.019897461, 2.0).astype(jnp.bfloat16),
    }


def reference(hologram, target):
    stride = WIN // 2
    energy = jnp.mean(hologram[0] * hologram[0] + hologram[1] * hologram[1]) + 1e-5
    padded = jnp.pad(hologram, ((0, 0), (0, stride), (0, stride)))
    ramp = (jnp.arange(WIN, dtype=jnp.float32) + 0.5) * (jnp.pi / WIN)
    profile = jnp.sin(ramp)
    window_taper = profile[:, None] * profile[None, :]

    def spectra(row_index):
        band_rows = lax.dynamic_slice_in_dim(padded, row_index * stride, WIN, axis=1)
        split_cols = band_rows.reshape(2, WIN, NWC + 1, stride)
        windows = jnp.concatenate([split_cols[:, :, :-1], split_cols[:, :, 1:]], axis=-1)
        windows = windows.transpose(0, 2, 1, 3) * window_taper
        spectrum = jnp.fft.fft2(windows[0] + 1j * windows[1], norm="ortho")
        power = jnp.real(spectrum) ** 2 + jnp.imag(spectrum) ** 2
        levels = lax.dynamic_index_in_dim(target, row_index, 0, keepdims=False)
        levels = levels.astype(jnp.float32).reshape(NWC, WIN, WIN)
        return spectrum, power, levels

    def sums(row_index):
        spectrum, power, levels = spectra(row_index)
        return jnp.stack([jnp.sum(power * power), jnp.sum(levels * power)])

    row_ids = jnp.arange(NWR, dtype=jnp.int32)
    summed = jnp.sum(lax.map(sums, row_ids), axis=0)
    moment = summed[0] / energy - summed[1]

    def grads(row_index):
        spectrum, power, levels = spectra(row_index)
        weighted = (power / energy - levels) * spectrum
        adjoint = jnp.fft.ifft2(weighted, norm="ortho")
        pieces = jnp.stack([jnp.real(adjoint), jnp.imag(adjoint)]) * window_taper
        pieces = pieces.transpose(0, 2, 1, 3)
        left_part = jnp.pad(pieces[..., :stride], ((0, 0), (0, 0), (0, 1), (0, 0)))
        right_part = jnp.pad(pieces[..., stride:], ((0, 0), (0, 0), (1, 0), (0, 0)))
        row_grad = (left_part + right_part).reshape(2, WIN, NC + stride)[:, :, :NC]
        return row_grad[:, :stride], row_grad[:, stride:]

    upper_half, lower_half = lax.map(grads, row_ids)
    shifted = jnp.concatenate([jnp.zeros_like(lower_half[:1]), lower_half[:-1]], axis=0)
    combined = (upper_half + shifted).transpose(1, 0, 2, 3).reshape(2, NR, NC)
    return combined - (moment / (energy * energy * (NR * NC))) * hologram
```

```python
import jax
import jax.numpy as jnp
import ml_dtypes
import numpy as np
from jax import lax
from jax.experimental import pallas as pl
from jax.experimental.pallas import tpu as pltpu
from jax.sharding import PartitionSpec as P

WIN = 64
STRIDE = WIN // 2
LANES = 128
AXES = ("row", "col")
DEPTH_BITS = (1, 2, 3, 4)
PLANE_BITS = (0, 5, 6, 7, 8)
LEAD = 11 * 32 + 21
BF16 = jnp.bfloat16
F32 = jnp.float32
CELLS = 512.0 * 32768.0


def split_host(table):
    high = table.astype(np.float32).astype(ml_dtypes.bfloat16)
    low = (table - high.astype(np.float64)).astype(np.float32).astype(ml_dtypes.bfloat16)
    return high, low


def host_tables():
    index = np.arange(WIN)
    phase = (np.outer(index, index) % WIN) * (2.0 * np.pi / WIN)
    taper = np.sin((index + 0.5) * (np.pi / WIN)) / np.sqrt(WIN)
    cosine = np.cos(phase) * taper[None, :]
    sine = np.sin(phase) * taper[None, :]
    upper, lower = slice(0, STRIDE), slice(STRIDE, WIN)
    by_row = np.block(
        [
            [cosine[:, upper], sine[:, upper], cosine[:, lower], sine[:, lower]],
            [-sine[:, upper], cosine[:, upper], -sine[:, lower], cosine[:, lower]],
        ]
    )
    two = np.eye(2)
    by_col = np.block(
        [
            [np.kron(two, cosine.T), np.kron(two, -sine.T)],
            [np.kron(two, sine.T), np.kron(two, cosine.T)],
        ]
    )
    row_high, row_low = split_host(by_row)
    half = 2 * STRIDE
    forward_own = np.concatenate([row_high[:, :half], row_high[:, :half], row_low[:, :half]], axis=1)
    forward_next = np.concatenate([row_high[:, half:], row_high[:, half:], row_low[:, half:]], axis=1)
    adjoint_high, adjoint_low = row_high.T, row_low.T
    backward = np.concatenate([adjoint_high, adjoint_high, adjoint_low], axis=1)
    col_high, col_low = split_host(by_col)
    pick = np.zeros((2, 2, 32, 2, 2, 32, 2, 2, 2), np.float32)
    for j2 in range(2):
        for e in range(2):
            for kk in range(32):
                for kpar in range(2):
                    pick[j2, e, kk, kpar, kpar, kk, j2, :, e] = 1.0
    pick = pick.reshape(256, 512).astype(ml_dtypes.bfloat16)
    wide = np.zeros((128, 64), ml_dtypes.bfloat16)
    return np.concatenate(
        [
            np.concatenate([forward_own, wide], axis=1),
            np.concatenate([forward_next, wide], axis=1),
            backward[:, :256],
            np.concatenate([backward[:, 256:], wide, wide], axis=1),
            col_high, col_low, col_high.T, col_low.T,
            pick[:, :256], pick[:, 256:],
        ],
        axis=0,
    )


TABLE = host_tables()
OWN, NEXT, BACK, BACK_LOW = (slice(k * 128, (k + 1) * 128) for k in range(4))
COL_HIGH, COL_LOW, COL_HIGH_T, COL_LOW_T, PICK_SAME, PICK_OTHER = (slice(512 + k * 256, 768 + k * 256) for k in range(6))


def split(block):
    high = block.astype(BF16)
    return high, (block - high.astype(F32)).astype(BF16)


def mul(left, right):
    return jnp.dot(left, right, preferred_element_type=F32)


def stacked(block):
    high, low = split(block)
    return jnp.concatenate([high, low, high], axis=0)


def local_kernel(holo_ref, target_ref, table_ref, first_ref, levels_ref, partial_ref, energy_ref):
    holo = holo_ref[...]
    first_ref[...] = holo[:, :LANES]
    energy_ref[...] = jnp.sum((holo * holo).reshape(8, 8, 1024), axis=0)
    partial_ref[...] = mul(table_ref[OWN, :192], stacked(holo))
    lane = lax.broadcasted_iota(jnp.int32, (8, LANES), 1)
    row = lax.broadcasted_iota(jnp.int32, (8, LANES), 0)
    side = (row // 2) % 2
    here = (lane // WIN) == side
    same, other = [], []
    for kk in range(32):
        tile = target_ref[:, kk * LANES:(kk + 1) * LANES].astype(F32)
        turned = pltpu.roll(tile, WIN, axis=1)
        parts_same, parts_other = [], []
        for g in range(4):
            plain = tile[8 * g:8 * g + 8]
            moved = turned[8 * g:8 * g + 8]
            parts_same.append(jnp.where(here, jnp.where(side == 0, plain, moved), 0.0))
            parts_other.append(jnp.where(here, jnp.where(side == 0, moved, plain), 0.0))
        same.append(jnp.concatenate(parts_same, axis=1))
        other.append(jnp.concatenate(parts_other, axis=1))
    gathered = jnp.concatenate(same + other, axis=0).astype(BF16)
    placed = mul(table_ref[PICK_SAME, :], gathered[:256]) + mul(table_ref[PICK_OTHER, :], gathered[256:])
    for g in range(4):
        for j2 in range(2):
            for e in range(2):
                start = (e * 8 + 2 * g + j2) * WIN
                source = (j2 * 2 + e) * WIN
                levels_ref[start:start + WIN, :] = placed[source:source + WIN, g * LANES:(g + 1) * LANES]


def window_kernel(
    side_ref, main_ref, levels_ref, energy_ref,
    table_ref,
    own_ref, rows_ref, tail_ref, sums_ref,
    high_ref, low_ref, grid_ref,
):
    main = main_ref[...]
    edge = mul(table_ref[OWN, :192], stacked(side_ref[:WIN])) + mul(
        table_ref[NEXT, :192], stacked(side_ref[WIN:])
    )
    wide = jnp.concatenate([main, edge], axis=1)
    shifted = pltpu.roll(wide, 1152 - STRIDE, axis=1)
    for e, field in enumerate((wide, shifted)):
        high, low = split(field)
        for j in range(8):
            at = slice((e * 8 + j) * WIN, (e * 8 + j + 1) * WIN)
            cols = slice(j * LANES, (j + 1) * LANES)
            for c in range(2):
                to = slice(c * LANES, (c + 1) * LANES)
                high_ref[at, to] = high[c * WIN:(c + 1) * WIN, cols]
                low_ref[at, to] = low[c * WIN:(c + 1) * WIN, cols]
    high, low = high_ref[...], low_ref[...]
    spectrum = mul(high, table_ref[COL_HIGH, :]) + mul(low, table_ref[COL_HIGH, :]) + mul(high, table_ref[COL_LOW, :])
    real, imag = spectrum[:, :LANES], spectrum[:, LANES:]
    power = real * real + imag * imag
    levels = levels_ref[...]
    squares = jnp.sum(power * power)
    crosses = jnp.sum(levels * power)
    energy = jnp.sum(energy_ref[...])
    lane = lax.broadcasted_iota(jnp.int32, (1, LANES), 1)
    sums_ref[...] = jnp.where(lane == 0, energy, jnp.where(lane == 1, squares, crosses))
    for v, factor in enumerate((power, levels)):
        high, low = split(jnp.concatenate([real * factor, imag * factor], axis=1))
        cols = mul(high, table_ref[COL_HIGH_T, :]) + mul(low, table_ref[COL_HIGH_T, :])
        cols = cols + mul(high, table_ref[COL_LOW_T, :])
        for c in range(2):
            at = slice(c * WIN, (c + 1) * WIN)
            lanes = slice(c * LANES, (c + 1) * LANES)
            even = [cols[j * WIN:(j + 1) * WIN, lanes] for j in range(8)]
            odd = [cols[(8 + j) * WIN:(9 + j) * WIN, lanes] for j in range(8)]
            zero = jnp.zeros((WIN, LANES), F32)
            grid_ref[at, :] = jnp.concatenate(even + [zero], axis=1) + pltpu.roll(
                jnp.concatenate(odd + [zero], axis=1), STRIDE, axis=1
            )
        high, low = split(grid_ref[...])
        result = mul(table_ref[BACK, :], jnp.concatenate([high, low], axis=0)) + mul(table_ref[BACK_LOW, :128], high)
        own_ref[v] = result[:WIN, :1024]
        tail_ref[v] = result[:WIN, 1024:]
        rows_ref[v] = result[WIN:, :]


def vmem(count):
    return [pl.BlockSpec(memory_space=pltpu.VMEM)] * count


def local_part(holo, target):
    return pl.pallas_call(
        local_kernel,
        out_shape=(
            jax.ShapeDtypeStruct((WIN, LANES), F32),
            jax.ShapeDtypeStruct((1024, LANES), F32),
            jax.ShapeDtypeStruct((128, 1024), F32),
            jax.ShapeDtypeStruct((8, 1024), F32),
        ),
        in_specs=vmem(3),
        out_specs=tuple(vmem(4)),
        compiler_params=pltpu.CompilerParams(vmem_limit_bytes=24 * 1024 * 1024),
        cost_estimate=pl.CostEstimate(flops=10**8, bytes_accessed=3 * 10**6, transcendentals=0),
        name="local_part",
    )(holo, target, TABLE)


def main_kernel(below_ref, partial_ref, table_ref, main_ref):
    main_ref[...] = partial_ref[...] + mul(table_ref[NEXT, :192], stacked(below_ref[...]))


def main_part(below, partial):
    return pl.pallas_call(
        main_kernel,
        out_shape=jax.ShapeDtypeStruct((128, 1024), F32),
        in_specs=vmem(3),
        out_specs=vmem(1)[0],
        compiler_params=pltpu.CompilerParams(vmem_limit_bytes=16 * 1024 * 1024),
        cost_estimate=pl.CostEstimate(flops=10**8, bytes_accessed=2 * 10**6, transcendentals=0),
        name="main_part",
    )(below, partial, TABLE)


def window_part(*operands):
    return pl.pallas_call(
        window_kernel,
        out_shape=(
            jax.ShapeDtypeStruct((2, WIN, 1024), F32),
            jax.ShapeDtypeStruct((2, WIN, 1152), F32),
            jax.ShapeDtypeStruct((2, WIN, LANES), F32),
            jax.ShapeDtypeStruct((1, LANES), F32),
        ),
        in_specs=vmem(5),
        out_specs=tuple(vmem(4)),
        scratch_shapes=[
            pltpu.VMEM((1024, 256), BF16),
            pltpu.VMEM((1024, 256), BF16),
            pltpu.VMEM((128, 1152), F32),
        ],
        compiler_params=pltpu.CompilerParams(vmem_limit_bytes=32 * 1024 * 1024),
        cost_estimate=pl.CostEstimate(flops=10**9, bytes_accessed=5 * 10**6, transcendentals=0),
        name="window_part",
    )(*operands, TABLE)


def combine_kernel(own_ref, rows_ref, cols_ref, holo_ref, sums_ref, out_ref):
    total = jnp.sum(sums_ref[...], axis=0, keepdims=True)
    energy = total[:, 0:1] / CELLS + 1e-5
    moment = total[:, 1:2] / energy - total[:, 2:3]
    inverse = 1.0 / energy
    slope = moment / (energy * energy * CELLS)
    first = own_ref[0] + rows_ref[0, :, :1024]
    second = own_ref[1] + rows_ref[1, :, :1024]
    out_ref[...] = first * inverse - second - slope * holo_ref[...]
    out_ref[:, :LANES] += cols_ref[0] * inverse - cols_ref[1]


def combine(own, rows, cols, holo, sums):
    return pl.pallas_call(
        combine_kernel,
        out_shape=jax.ShapeDtypeStruct((WIN, 1024), F32),
        in_specs=vmem(5),
        out_specs=vmem(1)[0],
        compiler_params=pltpu.CompilerParams(vmem_limit_bytes=16 * 1024 * 1024),
        cost_estimate=pl.CostEstimate(flops=10**6, bytes_accessed=2 * 10**6, transcendentals=0),
        name="combine",
    )(own, rows, cols, holo, sums)


def moved(block, rows, cols):
    row_size, col_size = lax.axis_size("row"), lax.axis_size("col")
    route = [
        (r * col_size + c, (r + rows) * col_size + c + cols)
        for r in range(row_size)
        for c in range(col_size)
        if 0 <= r + rows < row_size and 0 <= c + cols < col_size
    ]
    return lax.ppermute(block, AXES, route)


def shared(values, bits):
    masks = [0]
    for bit in bits:
        masks = masks + [mask ^ (1 << bit) for mask in masks]
    every = masks[-1]
    order = [mask ^ (LEAD & every) for mask in masks]
    groups = [[base | mask for mask in order] for base in range(512) if base & every == 0]
    copies = jnp.broadcast_to(values[None], (len(masks), 1, LANES))
    return lax.all_to_all(copies, AXES, 0, 0, axis_index_groups=groups, tiled=True)


def per_device(hologram, target):
    holo = hologram.reshape(WIN, 1024)
    below = moved(holo, -1, 0)
    first, levels, partial, energy = local_part(holo, target.reshape(32, 4096))
    side = moved(jnp.concatenate([first, below[:, :LANES]], axis=0), 0, -1)
    main = main_part(below, partial)
    own, rows, tail, sums = window_part(side, main, levels, energy)
    rows = moved(rows, 1, 0)
    sums = jnp.sum(shared(sums, DEPTH_BITS), axis=0)
    rows, sums = lax.optimization_barrier((rows, sums))
    cols = moved(tail + rows[:, :, 1024:], 0, 1)
    sums = shared(sums, PLANE_BITS).reshape(32, LANES)
    return combine(own, rows, cols, holo, sums).reshape(2, STRIDE, 1024)


def solution(mesh):
    return jax.shard_map(
        per_device,
        mesh=mesh,
        in_specs=(P(None, "row", "col"), P("row", "col", None)),
        out_specs=P(None, "row", "col"),
        check_vma=False,
    )
```

```python
import jax
import jax.numpy as jnp
import ml_dtypes
import numpy as np
from jax import lax
from jax.experimental import pallas as pl
from jax.experimental.pallas import tpu as pltpu
from jax.sharding import PartitionSpec as P

WIN = 64
STRIDE = WIN // 2
LANES = 128
AXES = ("row", "col")
DEPTH_BITS = (5, 1, 2, 3, 4)
PLANE_BITS = (0, 6, 7, 8)
LEAD = 11 * 32 + 21
BF16 = jnp.bfloat16
F32 = jnp.float32
CELLS = 512.0 * 32768.0
MERGE_BYTES = 300000


def split_host(table):
    high = table.astype(np.float32).astype(ml_dtypes.bfloat16)
    low = (table - high.astype(np.float64)).astype(np.float32).astype(ml_dtypes.bfloat16)
    return high, low


def host_tables():
    index = np.arange(WIN)
    phase = (np.outer(index, index) % WIN) * (2.0 * np.pi / WIN)
    taper = np.sin((index + 0.5) * (np.pi / WIN)) / np.sqrt(WIN)
    cosine = np.cos(phase) * taper[None, :]
    sine = np.sin(phase) * taper[None, :]
    upper, lower = slice(0, STRIDE), slice(STRIDE, WIN)
    by_row = np.block(
        [
            [cosine[:, upper], sine[:, upper], cosine[:, lower], sine[:, lower]],
            [-sine[:, upper], cosine[:, upper], -sine[:, lower], cosine[:, lower]],
        ]
    )
    two = np.eye(2)
    by_col = np.block(
        [
            [np.kron(two, cosine.T), np.kron(two, -sine.T)],
            [np.kron(two, sine.T), np.kron(two, cosine.T)],
        ]
    )
    row_high, row_low = split_host(by_row)
    half = 2 * STRIDE
    forward_own = np.concatenate([row_high[:, :half], row_high[:, :half], row_low[:, :half]], axis=1)
    forward_next = np.concatenate([row_high[:, half:], row_high[:, half:], row_low[:, half:]], axis=1)
    adjoint_high, adjoint_low = row_high.T, row_low.T
    backward = np.concatenate([adjoint_high, adjoint_high, adjoint_low], axis=1)
    col_high, col_low = split_host(by_col)
    pick = np.zeros((2, 2, 32, 2, 2, 32, 2, 2, 2), np.float32)
    for j2 in range(2):
        for e in range(2):
            for kk in range(32):
                for kpar in range(2):
                    pick[j2, e, kk, kpar, kpar, kk, j2, :, e] = 1.0
    pick = pick.reshape(256, 512).astype(ml_dtypes.bfloat16)
    wide = np.zeros((128, 64), ml_dtypes.bfloat16)
    return np.concatenate(
        [
            np.concatenate([forward_own, wide], axis=1),
            np.concatenate([forward_next, wide], axis=1),
            backward[:, :256],
            np.concatenate([backward[:, 256:], wide, wide], axis=1),
            col_high, col_low, col_high.T, col_low.T,
            pick[:, :256], pick[:, 256:],
        ],
        axis=0,
    )


TABLE = host_tables()
OWN, NEXT, BACK, BACK_LOW = (slice(k * 128, (k + 1) * 128) for k in range(4))
COL_HIGH, COL_LOW, COL_HIGH_T, COL_LOW_T, PICK_SAME, PICK_OTHER = (slice(512 + k * 256, 768 + k * 256) for k in range(6))


def split(block):
    high = block.astype(BF16)
    return high, (block - high.astype(F32)).astype(BF16)


def mul(left, right):
    return jnp.dot(left, right, preferred_element_type=F32)


def stacked(block):
    high, low = split(block)
    return jnp.concatenate([high, low, high], axis=0)


def local_kernel(
    holo_hbm, target_hbm, table_hbm, holo_ref, table_ref, levels_ref, partial_ref, energy_ref, target_ref, sems
):
    copies = [
        pltpu.make_async_copy(source, place, sems.at[k])
        for k, (source, place) in enumerate(
            [(holo_hbm, holo_ref), (table_hbm, table_ref), (target_hbm, target_ref)]
        )
    ]
    for copy in copies:
        copy.start()
    copies[0].wait()
    holo = holo_ref[...]
    energy_ref[...] = jnp.sum((holo * holo).reshape(8, 8, 1024), axis=0)
    field = stacked(holo)
    copies[1].wait()
    partial_ref[...] = mul(table_ref[OWN, :192], field)
    copies[2].wait()
    lane = lax.broadcasted_iota(jnp.int32, (8, LANES), 1)
    row = lax.broadcasted_iota(jnp.int32, (8, LANES), 0)
    side = (row // 2) % 2
    here = (lane // WIN) == side
    same, other = [], []
    for kk in range(32):
        tile = target_ref[:, kk * LANES:(kk + 1) * LANES].astype(F32)
        turned = pltpu.roll(tile, WIN, axis=1)
        parts_same, parts_other = [], []
        for g in range(4):
            plain = tile[8 * g:8 * g + 8]
            moved = turned[8 * g:8 * g + 8]
            parts_same.append(jnp.where(here, jnp.where(side == 0, plain, moved), 0.0))
            parts_other.append(jnp.where(here, jnp.where(side == 0, moved, plain), 0.0))
        same.append(jnp.concatenate(parts_same, axis=1))
        other.append(jnp.concatenate(parts_other, axis=1))
    gathered = jnp.concatenate(same + other, axis=0).astype(BF16)
    placed = mul(table_ref[PICK_SAME, :], gathered[:256]) + mul(table_ref[PICK_OTHER, :], gathered[256:])
    for g in range(4):
        for j2 in range(2):
            for e in range(2):
                start = (e * 8 + 2 * g + j2) * WIN
                source = (j2 * 2 + e) * WIN
                levels_ref[start:start + WIN, :] = placed[source:source + WIN, g * LANES:(g + 1) * LANES]


def along_cols(high, low, table_ref, high_at, low_at):
    table = jnp.concatenate([table_ref[high_at, :], table_ref[high_at, :], table_ref[low_at, :]], axis=0)
    return mul(jnp.concatenate([high, low, high], axis=1), table)


def window_kernel(
    below_ref, right_ref, corner_ref, table_ref, levels_ref, partial_ref, energy_ref,
    own_ref, rows_ref, tail_ref, sums_hbm,
    high_ref, low_ref, grid_ref, copies_ref, sem,
):
    main = partial_ref[...] + mul(table_ref[NEXT, :192], stacked(below_ref[...]))
    edge = mul(table_ref[OWN, :192], stacked(right_ref[...])) + mul(table_ref[NEXT, :192], stacked(corner_ref[...]))
    wide = jnp.concatenate([main, edge], axis=1)
    shifted = pltpu.roll(wide, 1152 - STRIDE, axis=1)
    for e, field in enumerate((wide, shifted)):
        high, low = split(field)
        for j in range(8):
            at = slice((e * 8 + j) * WIN, (e * 8 + j + 1) * WIN)
            cols = slice(j * LANES, (j + 1) * LANES)
            for c in range(2):
                to = slice(c * LANES, (c + 1) * LANES)
                high_ref[at, to] = high[c * WIN:(c + 1) * WIN, cols]
                low_ref[at, to] = low[c * WIN:(c + 1) * WIN, cols]
    spectrum = along_cols(high_ref[...], low_ref[...], table_ref, COL_HIGH, COL_LOW)
    real, imag = spectrum[:, :LANES], spectrum[:, LANES:]
    power = real * real + imag * imag
    levels = levels_ref[...]
    squares = jnp.sum(power * power)
    crosses = jnp.sum(levels * power)
    energy = jnp.sum(energy_ref[...])
    lane = lax.broadcasted_iota(jnp.int32, (1, LANES), 1)
    row = jnp.where(lane == 0, energy, jnp.where(lane == 1, squares, crosses))
    copies_ref[...] = jnp.broadcast_to(row[None], copies_ref.shape)
    copy = pltpu.make_async_copy(copies_ref, sums_hbm, sem)
    for v, factor in enumerate((power, levels)):
        high, low = split(jnp.concatenate([real * factor, imag * factor], axis=1))
        cols = along_cols(high, low, table_ref, COL_HIGH_T, COL_LOW_T)
        for c in range(2):
            at = slice(c * WIN, (c + 1) * WIN)
            lanes = slice(c * LANES, (c + 1) * LANES)
            even = [cols[j * WIN:(j + 1) * WIN, lanes] for j in range(8)]
            odd = [cols[(8 + j) * WIN:(9 + j) * WIN, lanes] for j in range(8)]
            zero = jnp.zeros((WIN, LANES), F32)
            grid_ref[at, :] = jnp.concatenate(even + [zero], axis=1) + pltpu.roll(
                jnp.concatenate(odd + [zero], axis=1), STRIDE, axis=1
            )
        if v == 1:
            copy.start()
        result = mul(jnp.concatenate([table_ref[BACK, :], table_ref[BACK_LOW, :128]], axis=1), stacked(grid_ref[...]))
        own_ref[v] = result[:WIN, :1024]
        tail_ref[v] = result[:WIN, 1024:]
        rows_ref[v] = result[WIN:, :]
    copy.wait()


def vmem(count):
    return [pl.BlockSpec(memory_space=pltpu.VMEM)] * count


def local_part(*operands):
    return pl.pallas_call(
        local_kernel,
        out_shape=(
            pltpu.VMEM((WIN, 1024), F32),
            pltpu.VMEM(TABLE.shape, BF16),
            pltpu.VMEM((1024, LANES), F32),
            pltpu.VMEM((128, 1024), F32),
            pltpu.VMEM((8, 1024), F32),
        ),
        in_specs=[pl.BlockSpec(memory_space=pl.ANY)] * 3,
        out_specs=tuple(vmem(5)),
        scratch_shapes=[pltpu.VMEM((32, 4096), BF16), pltpu.SemaphoreType.DMA((3,))],
        compiler_params=pltpu.CompilerParams(vmem_limit_bytes=24 * 1024 * 1024),
        cost_estimate=pl.CostEstimate(flops=10**8, bytes_accessed=3 * 10**6, transcendentals=0),
        name="local_part",
    )(*(pltpu.with_memory_space_constraint(operand, pltpu.HBM) for operand in operands))


def window_part(*operands):
    return pl.pallas_call(
        window_kernel,
        out_shape=(
            jax.ShapeDtypeStruct((2, WIN, 1024), F32),
            jax.ShapeDtypeStruct((2, WIN, 1152), F32),
            jax.ShapeDtypeStruct((2, WIN, LANES), F32),
            pltpu.HBM((32, 1, LANES), F32),
        ),
        in_specs=vmem(7),
        out_specs=tuple(vmem(3)) + (pl.BlockSpec(memory_space=pl.ANY),),
        scratch_shapes=[
            pltpu.VMEM((1024, 256), BF16),
            pltpu.VMEM((1024, 256), BF16),
            pltpu.VMEM((128, 1152), F32),
            pltpu.VMEM((32, 1, LANES), F32),
            pltpu.SemaphoreType.DMA,
        ],
        compiler_params=pltpu.CompilerParams(vmem_limit_bytes=32 * 1024 * 1024),
        cost_estimate=pl.CostEstimate(flops=10**9, bytes_accessed=5 * 10**6, transcendentals=0),
        name="window_part",
    )(*operands)


def merge_kernel(own_ref, rows_ref, both_ref):
    both_ref[...] = own_ref[...] + rows_ref[:, :, :1024]


def merge_part(own, rows):
    return pl.pallas_call(
        merge_kernel,
        out_shape=pltpu.VMEM((2, WIN, 1024), F32),
        in_specs=vmem(2),
        out_specs=vmem(1)[0],
        compiler_params=pltpu.CompilerParams(vmem_limit_bytes=16 * 1024 * 1024),
        cost_estimate=pl.CostEstimate(flops=10**6, bytes_accessed=MERGE_BYTES, transcendentals=0),
        name="merge_part",
    )(own, rows)


def combine_kernel(both_ref, edge_ref, holo_ref, sums_ref, out_ref):
    total = jnp.sum(sums_ref[...], axis=0, keepdims=True)
    energy = total[:, 0:1] / CELLS + 1e-5
    moment = total[:, 1:2] / energy - total[:, 2:3]
    inverse = 1.0 / energy
    slope = moment / (energy * energy * CELLS)
    out_ref[...] = both_ref[0] * inverse - both_ref[1] - slope * holo_ref[...]
    out_ref[:, :LANES] += edge_ref[0] * inverse - edge_ref[1]


def combine(*operands):
    return pl.pallas_call(
        combine_kernel,
        out_shape=jax.ShapeDtypeStruct((WIN, 1024), F32),
        in_specs=vmem(4),
        out_specs=vmem(1)[0],
        compiler_params=pltpu.CompilerParams(vmem_limit_bytes=16 * 1024 * 1024),
        cost_estimate=pl.CostEstimate(flops=10**6, bytes_accessed=2 * 10**6, transcendentals=0),
        name="combine",
    )(*operands)


def moved(block, rows, cols):
    row_size, col_size = lax.axis_size("row"), lax.axis_size("col")
    route = [
        (r * col_size + c, (r + rows) * col_size + c + cols)
        for r in range(row_size)
        for c in range(col_size)
        if 0 <= r + rows < row_size and 0 <= c + cols < col_size
    ]
    return lax.ppermute(block, AXES, route)


def shared(values, bits):
    masks = [0]
    for bit in bits:
        masks = masks + [mask ^ (1 << bit) for mask in masks]
    every = masks[-1]
    order = [mask ^ (LEAD & every) for mask in masks]
    groups = [[base | mask for mask in order] for base in range(512) if base & every == 0]
    copies = values
    if copies.ndim == 2:
        copies = jnp.broadcast_to(values[None], (len(masks), 1, LANES))
    return lax.all_to_all(copies, AXES, 0, 0, axis_index_groups=groups, tiled=True)


def per_device(hologram, target):
    holo = hologram.reshape(WIN, 1024)
    below = moved(holo, -1, 0)
    first = holo[:, :LANES]
    corner = moved(first, -1, -1)
    right = moved(first, 0, -1)
    holo, *local = local_part(holo, target.reshape(32, 4096), TABLE)
    own, rows, tail, sums = window_part(below, right, corner, *local)
    rows = moved(rows, 1, 0)
    edge = moved(tail + rows[:, :, 1024:], 0, 1)
    sums = jnp.sum(shared(sums, DEPTH_BITS), axis=0)
    both = merge_part(own, rows)
    both, sums = lax.optimization_barrier((both, sums))
    sums = shared(sums, PLANE_BITS).reshape(-1, LANES)
    return combine(both, edge, holo, sums).reshape(2, STRIDE, 1024)


def solution(mesh):
    return jax.shard_map(
        per_device,
        mesh=mesh,
        in_specs=(P(None, "row", "col"), P("row", "col", None)),
        out_specs=P(None, "row", "col"),
        check_vma=False,
    )
```

```python
import jax
import jax.numpy as jnp
import ml_dtypes
import numpy as np
from jax import lax
from jax.experimental import pallas as pl
from jax.experimental.pallas import tpu as pltpu
from jax.sharding import PartitionSpec as P

WIN = 64
STRIDE = WIN // 2
LANES = 128
AXES = ("row", "col")
DEPTH_BITS = (5, 1, 2, 3, 4)
PLANE_BITS = (0, 6, 7, 8)
LEAD = 11 * 32 + 21
BF16 = jnp.bfloat16
F32 = jnp.float32
CELLS = 512.0 * 32768.0
INNER = 15 * WIN
MERGE_BYTES = 300000
ZERO_FLOPS = 10**10


def split_host(table):
    high = table.astype(np.float32).astype(ml_dtypes.bfloat16)
    low = (table - high.astype(np.float64)).astype(np.float32).astype(ml_dtypes.bfloat16)
    return high, low


def host_tables():
    index = np.arange(WIN)
    phase = (np.outer(index, index) % WIN) * (2.0 * np.pi / WIN)
    taper = np.sin((index + 0.5) * (np.pi / WIN)) / np.sqrt(WIN)
    cosine = np.cos(phase) * taper[None, :]
    sine = np.sin(phase) * taper[None, :]
    upper, lower = slice(0, STRIDE), slice(STRIDE, WIN)
    by_row = np.block(
        [
            [cosine[:, upper], sine[:, upper], cosine[:, lower], sine[:, lower]],
            [-sine[:, upper], cosine[:, upper], -sine[:, lower], cosine[:, lower]],
        ]
    )
    two = np.eye(2)
    by_col = np.block(
        [
            [np.kron(two, cosine.T), np.kron(two, -sine.T)],
            [np.kron(two, sine.T), np.kron(two, cosine.T)],
        ]
    )
    row_high, row_low = split_host(by_row)
    half = 2 * STRIDE
    col_high, col_low = split_host(by_col)
    return np.concatenate(
        [
            two_level(row_high[:, :half], row_low[:, :half], 256),
            two_level(row_high[:, half:], row_low[:, half:], 256),
            two_level(row_high, row_low, 256),
            two_level(row_high.T, row_low.T, 256),
            col_high, col_low,
        ],
        axis=0,
    )


def two_level(high, low, width):
    pad = np.zeros((high.shape[0], width - 2 * high.shape[1]), high.dtype)
    upper = np.concatenate([high, high, pad], axis=1)
    lower = np.concatenate([low, np.zeros_like(low), pad], axis=1)
    return np.concatenate([upper, lower], axis=0)


TABLE = host_tables()
OWN, NEXT, BOTH, BACK, COL_HIGH, COL_LOW = (slice(k * 256, (k + 1) * 256) for k in range(6))


def split(block):
    high = block.astype(BF16)
    return high, (block - high.astype(F32)).astype(BF16)


def mul(left, right):
    return jnp.dot(left, right, preferred_element_type=F32)


def by_rows(table, block):
    high, low = split(block)
    both = mul(table, jnp.concatenate([high, low], axis=0))
    return both[:128] + both[128:]


def turned(tiles):
    lane = lax.broadcasted_iota(jnp.int32, tiles[0].shape, 1)
    moved_tiles = [pltpu.roll(tile, STRIDE, axis=1) for tile in tiles]
    zero = jnp.zeros_like(tiles[0])
    return [
        jnp.where(lane < STRIDE, before, after)
        for before, after in zip([zero] + moved_tiles, moved_tiles + [zero])
    ]


def zero_kernel(out_ref):
    out_ref[...] = jnp.zeros_like(out_ref)


def zero_part():
    return pl.pallas_call(
        zero_kernel,
        out_shape=pltpu.VMEM((8, LANES), F32),
        out_specs=vmem(1)[0],
        compiler_params=pltpu.CompilerParams(vmem_limit_bytes=16 * 1024 * 1024),
        cost_estimate=pl.CostEstimate(flops=ZERO_FLOPS, bytes_accessed=4096, transcendentals=0),
        name="zero_part",
    )()


def first_kernel(holo_ref, zero_ref, out_ref):
    out_ref[...] = holo_ref[:, :LANES]


def first_part(holo, zero):
    return pl.pallas_call(
        first_kernel,
        out_shape=pltpu.VMEM((WIN, LANES), F32),
        in_specs=vmem(2),
        out_specs=vmem(1)[0],
        compiler_params=pltpu.CompilerParams(vmem_limit_bytes=16 * 1024 * 1024),
        cost_estimate=pl.CostEstimate(flops=0, bytes_accessed=4 * 10**5, transcendentals=0),
        name="first_part",
    )(holo, zero)


def local_kernel(holo_ref, target_ref, table_ref, levels_ref, partial_ref, energy_ref):
    pick = jnp.concatenate(picks(), axis=1)
    holo = holo_ref[...]
    energy = jnp.sum((holo * holo).reshape(8, 8, 1024), axis=0)
    energy_ref[...] = sum(energy[:, k * LANES:(k + 1) * LANES] for k in range(8))
    partial_ref[...] = by_rows(table_ref[OWN, :128], holo)
    lane = lax.broadcasted_iota(jnp.int32, (8, LANES), 1)
    row = lax.broadcasted_iota(jnp.int32, (8, LANES), 0)
    side = (row // 2) % 2
    here = (lane // WIN) == side
    same, other = [], []
    for kk in range(32):
        tile = target_ref[:, kk * LANES:(kk + 1) * LANES].astype(F32)
        turned = pltpu.roll(tile, WIN, axis=1)
        parts_same, parts_other = [], []
        for g in range(4):
            plain = tile[8 * g:8 * g + 8]
            moved = turned[8 * g:8 * g + 8]
            parts_same.append(jnp.where(here, jnp.where(side == 0, plain, moved), 0.0))
            parts_other.append(jnp.where(here, jnp.where(side == 0, moved, plain), 0.0))
        same.append(jnp.concatenate(parts_same, axis=1))
        other.append(jnp.concatenate(parts_other, axis=1))
    gathered = jnp.concatenate(same + other, axis=0).astype(BF16)
    placed = mul(pick, gathered)
    for g in range(4):
        for j2 in range(2):
            for e in range(2):
                start = (e * 8 + 2 * g + j2) * WIN
                source = (j2 * 2 + e) * WIN
                levels_ref[start:start + WIN, :] = placed[source:source + WIN, g * LANES:(g + 1) * LANES]


def along_cols(high, low, table_ref):
    table = jnp.concatenate([table_ref[COL_HIGH, :], table_ref[COL_HIGH, :], table_ref[COL_LOW, :]], axis=0)
    return mul(jnp.concatenate([high, low, high], axis=1), table)


def back_cols(high, low, table_ref):
    table = jnp.concatenate([table_ref[COL_HIGH, :], table_ref[COL_HIGH, :], table_ref[COL_LOW, :]], axis=1)
    fields = jnp.concatenate([high, low, high], axis=1)
    return lax.dot_general(fields, table, (((1,), (1,)), ((), ())), preferred_element_type=F32)


def picks():
    row = lax.broadcasted_iota(jnp.int32, (256, 256), 0)
    col = lax.broadcasted_iota(jnp.int32, (256, 256), 1)
    match = ((row >> 1) & 31) == (col >> 3)
    match = match & ((row >> 7) == ((col >> 2) & 1)) & (((row >> 6) & 1) == (col & 1))
    even = (row & 1) == 0
    return [jnp.where(match & side, 1.0, 0.0).astype(BF16) for side in (even, jnp.logical_not(even))]


def packed(*terms):
    sublane = lax.broadcasted_iota(jnp.int32, (8, LANES), 0)
    lane = lax.broadcasted_iota(jnp.int32, (8, LANES), 1)
    stack = jnp.zeros((8, LANES), F32)
    for k, term in enumerate(terms):
        stack = jnp.where(sublane == k, jnp.sum(term, axis=0, keepdims=True), stack)
    totals = jnp.sum(stack, axis=1, keepdims=True)
    return jnp.sum(jnp.where(lane == sublane, totals, 0.0), axis=0, keepdims=True)


def spread(fields, high_ref, low_ref, first):
    for j, field in enumerate(fields):
        at = slice((first + j) * WIN, (first + j + 1) * WIN)
        high, low = split(field)
        for c in range(2):
            to = slice(c * LANES, (c + 1) * LANES)
            high_ref[at, to] = high[c * WIN:(c + 1) * WIN]
            low_ref[at, to] = low[c * WIN:(c + 1) * WIN]


def back_by_stride(tiles):
    lane = lax.broadcasted_iota(jnp.int32, tiles[0].shape, 1)
    ahead = [pltpu.roll(tile, LANES - STRIDE, axis=1) for tile in tiles]
    return [jnp.where(lane < LANES - STRIDE, here, after) for here, after in zip(ahead[:-1], ahead[1:])]


def spectra(high_ref, low_ref, levels, table_ref):
    spectrum = along_cols(high_ref[...], low_ref[...], table_ref)
    real, imag = spectrum[:, :LANES], spectrum[:, LANES:]
    power = real * real + imag * imag
    return real, imag, power, packed(power * power, levels * power)


def adjoint_cols(real, imag, factor, table_ref):
    high, low = split(jnp.concatenate([real * factor, imag * factor], axis=1))
    return back_cols(high, low, table_ref)


def place(grid_ref, c, tile, at):
    high, low = split(tile)
    grid_ref[c * WIN:(c + 1) * WIN, at:at + LANES] = high
    grid_ref[128 + c * WIN:128 + (c + 1) * WIN, at:at + LANES] = low


def along_rows(grid_ref, table_ref):
    result = mul(table_ref[BACK, :], grid_ref[...])
    return result[:128] + result[128:]


def inner_kernel(
    below_ref, table_ref, levels_ref, partial_ref,
    own_ref, rows_ref, last_ref, sums_ref,
    high_ref, low_ref, grid_ref,
):
    main = partial_ref[...] + by_rows(table_ref[NEXT, :128], below_ref[...])
    tiles = [main[:, j * LANES:(j + 1) * LANES] for j in range(8)]
    last_ref[...] = tiles[7]
    spread(tiles, high_ref, low_ref, 0)
    spread(back_by_stride(tiles), high_ref, low_ref, 8)
    levels = levels_ref[:INNER, :]
    real, imag, power, sums_ref[...] = spectra(high_ref, low_ref, levels, table_ref)
    for v, factor in enumerate((power, levels)):
        cols = adjoint_cols(real, imag, factor, table_ref)
        for c in range(2):
            lanes = slice(c * LANES, (c + 1) * LANES)
            odd = turned([cols[(8 + j) * WIN:(9 + j) * WIN, lanes] for j in range(7)])
            for j in range(8):
                place(grid_ref, c, odd[j] + cols[j * WIN:(j + 1) * WIN, lanes], (v * 8 + j) * LANES)
    result = along_rows(grid_ref, table_ref)
    for v in range(2):
        own_ref[v] = result[:WIN, v * 1024:(v + 1) * 1024]
        rows_ref[v] = result[WIN:, v * 1024:(v + 1) * 1024]


def edge_kernel(
    right_ref, corner_ref, table_ref, levels_ref, energy_ref, last_ref, inner_ref, inner_sums_ref,
    edge_ref, rows_ref, copies_ref,
    high_ref, low_ref, grid_ref,
):
    edge = by_rows(table_ref[BOTH, :], jnp.concatenate([right_ref[...], corner_ref[...]], axis=0))
    spread(back_by_stride([last_ref[...], edge]), high_ref, low_ref, 0)
    levels = levels_ref[INNER:, :]
    real, imag, power, sums = spectra(high_ref, low_ref, levels, table_ref)
    row = inner_sums_ref[...] + sums + packed(jnp.zeros((8, LANES), F32), jnp.zeros((8, LANES), F32), energy_ref[...])
    copies_ref[...] = jnp.broadcast_to(row[None], copies_ref.shape)
    for v, factor in enumerate((power, levels)):
        cols = adjoint_cols(real, imag, factor, table_ref)
        for c in range(2):
            for j, tile in enumerate(turned([cols[:, c * LANES:(c + 1) * LANES]])):
                place(grid_ref, c, tile, (v * 2 + j) * LANES)
    result = along_rows(grid_ref, table_ref)
    for v in range(2):
        mine = result[:, v * 2 * LANES:(v + 1) * 2 * LANES]
        edge_ref[v] = mine[:WIN]
        rows_ref[v, :, :7 * LANES] = inner_ref[v, :, :7 * LANES]
        rows_ref[v, :, 7 * LANES:8 * LANES] = inner_ref[v, :, 7 * LANES:] + mine[WIN:, :LANES]
        rows_ref[v, :, 8 * LANES:] = mine[WIN:, LANES:]


def vmem(count):
    return [pl.BlockSpec(memory_space=pltpu.VMEM)] * count


def local_part(*operands):
    return pl.pallas_call(
        local_kernel,
        out_shape=(
            pltpu.VMEM((1024, LANES), F32),
            pltpu.VMEM((128, 1024), F32),
            pltpu.VMEM((8, LANES), F32),
        ),
        in_specs=vmem(3),
        out_specs=tuple(vmem(3)),
        compiler_params=pltpu.CompilerParams(vmem_limit_bytes=24 * 1024 * 1024),
        cost_estimate=pl.CostEstimate(flops=10**8, bytes_accessed=3 * 10**6, transcendentals=0),
        name="local_part",
    )(*operands)


def inner_part(*operands):
    return pl.pallas_call(
        inner_kernel,
        out_shape=(
            pltpu.VMEM((2, WIN, 1024), F32),
            pltpu.VMEM((2, WIN, 1024), F32),
            pltpu.VMEM((128, LANES), F32),
            pltpu.VMEM((1, LANES), F32),
        ),
        in_specs=vmem(4),
        out_specs=tuple(vmem(4)),
        scratch_shapes=[
            pltpu.VMEM((INNER, 256), BF16),
            pltpu.VMEM((INNER, 256), BF16),
            pltpu.VMEM((256, 16 * LANES), BF16),
        ],
        compiler_params=pltpu.CompilerParams(vmem_limit_bytes=32 * 1024 * 1024),
        cost_estimate=pl.CostEstimate(flops=10**9, bytes_accessed=5 * 10**6, transcendentals=0),
        name="inner_part",
    )(*operands)


def edge_part(*operands):
    return pl.pallas_call(
        edge_kernel,
        out_shape=(
            pltpu.VMEM((2, WIN, 256), F32),
            pltpu.VMEM((2, WIN, 1152), F32),
            pltpu.VMEM((32, 1, LANES), F32),
        ),
        in_specs=vmem(8),
        out_specs=tuple(vmem(3)),
        scratch_shapes=[
            pltpu.VMEM((WIN, 256), BF16),
            pltpu.VMEM((WIN, 256), BF16),
            pltpu.VMEM((256, 4 * LANES), BF16),
        ],
        compiler_params=pltpu.CompilerParams(vmem_limit_bytes=16 * 1024 * 1024),
        cost_estimate=pl.CostEstimate(flops=10**8, bytes_accessed=2 * 10**6, transcendentals=0),
        name="edge_part",
    )(*operands)


def merge_kernel(own_ref, edge_ref, rows_ref, both_ref):
    both_ref[:, :, :7 * LANES] = own_ref[:, :, :7 * LANES] + rows_ref[:, :, :7 * LANES]
    last = slice(7 * LANES, 8 * LANES)
    both_ref[:, :, last] = own_ref[:, :, last] + edge_ref[:, :, :LANES] + rows_ref[:, :, last]


def merge_part(*operands):
    return pl.pallas_call(
        merge_kernel,
        out_shape=pltpu.VMEM((2, WIN, 1024), F32),
        in_specs=vmem(3),
        out_specs=vmem(1)[0],
        compiler_params=pltpu.CompilerParams(vmem_limit_bytes=16 * 1024 * 1024),
        cost_estimate=pl.CostEstimate(flops=10**6, bytes_accessed=MERGE_BYTES, transcendentals=0),
        name="merge_part",
    )(*operands)


def combine_kernel(both_ref, cols_ref, holo_ref, sums_ref, out_hbm, out_ref, sems):
    total = jnp.sum(sums_ref[...], axis=0, keepdims=True)
    energy = total[:, 2:3] / CELLS + 1e-5
    moment = total[:, 0:1] / energy - total[:, 1:2]
    inverse = 1.0 / energy
    slope = moment / (energy * energy * CELLS)
    copies = []
    for k in range(4):
        at = slice(k * 16, (k + 1) * 16)
        out_ref[at, :] = both_ref[0, at] * inverse - both_ref[1, at] - slope * holo_ref[at, :]
        out_ref[at, :LANES] += cols_ref[0, at] * inverse - cols_ref[1, at]
        copy = pltpu.make_async_copy(out_ref.at[pl.ds(k * 16, 16)], out_hbm.at[pl.ds(k * 16, 16)], sems.at[k])
        copy.start()
        copies.append(copy)
    for copy in copies:
        copy.wait()


def combine(*operands):
    return pl.pallas_call(
        combine_kernel,
        out_shape=pltpu.HBM((WIN, 1024), F32),
        in_specs=vmem(4),
        out_specs=pl.BlockSpec(memory_space=pl.ANY),
        scratch_shapes=[pltpu.VMEM((WIN, 1024), F32), pltpu.SemaphoreType.DMA((4,))],
        compiler_params=pltpu.CompilerParams(vmem_limit_bytes=16 * 1024 * 1024),
        cost_estimate=pl.CostEstimate(flops=10**6, bytes_accessed=2 * 10**6, transcendentals=0),
        name="combine",
    )(*operands)


def moved(block, rows, cols):
    row_size, col_size = lax.axis_size("row"), lax.axis_size("col")
    route = [
        (r * col_size + c, (r + rows) * col_size + c + cols)
        for r in range(row_size)
        for c in range(col_size)
        if 0 <= r + rows < row_size and 0 <= c + cols < col_size
    ]
    return lax.ppermute(block, AXES, route)


def shared(values, bits):
    masks = [0]
    for bit in bits:
        masks = masks + [mask ^ (1 << bit) for mask in masks]
    every = masks[-1]
    order = [mask ^ (LEAD & every) for mask in masks]
    groups = [[base | mask for mask in order] for base in range(512) if base & every == 0]
    copies = values
    if copies.ndim == 2:
        copies = jnp.broadcast_to(values[None], (len(masks), 1, LANES))
    return lax.all_to_all(copies, AXES, 0, 0, axis_index_groups=groups, tiled=True)


def per_device(hologram, target):
    holo = hologram.reshape(WIN, 1024)
    below = moved(holo, -1, 0)
    first = first_part(holo, zero_part())
    corner = moved(first, -1, -1)
    right = moved(first, 0, -1)
    levels, partial, energy = local_part(holo, target.reshape(32, 4096), TABLE)
    own, inner, last, sums = inner_part(below, TABLE, levels, partial)
    edge, rows, sums = edge_part(right, corner, TABLE, levels, energy, last, inner, sums)
    rows = moved(rows, 1, 0)
    cols = moved(edge[:, :, LANES:] + rows[:, :, 1024:], 0, 1)
    sums = jnp.sum(shared(sums, DEPTH_BITS), axis=0)
    both = merge_part(own, edge, rows)
    both, sums = lax.optimization_barrier((both, sums))
    sums = shared(sums, PLANE_BITS).reshape(-1, LANES)
    return combine(both, cols, holo, sums).reshape(2, STRIDE, 1024)


def solution(mesh):
    return jax.shard_map(
        per_device,
        mesh=mesh,
        in_specs=(P(None, "row", "col"), P("row", "col", None)),
        out_specs=P(None, "row", "col"),
        check_vma=False,
    )
```

```python
import jax
import jax.numpy as jnp
import ml_dtypes
import numpy as np
from jax import lax
from jax.experimental import pallas as pl
from jax.experimental.pallas import tpu as pltpu
from jax.sharding import PartitionSpec as P

WIN = 64
STRIDE = WIN // 2
LANES = 128
AXES = ("row", "col")
DEPTH_BITS = (5, 1, 2, 3, 4)
PLANE_BITS = (0, 6, 7, 8)
LEAD = 11 * 32 + 20
BF16 = jnp.bfloat16
F32 = jnp.float32
CELLS = 512.0 * 32768.0
INNER = 15 * WIN
MERGE_BYTES = 300000
ZERO_FLOPS = 10**10


def split_host(table):
    high = table.astype(np.float32).astype(ml_dtypes.bfloat16)
    low = (table - high.astype(np.float64)).astype(np.float32).astype(ml_dtypes.bfloat16)
    return high, low


def host_tables():
    index = np.arange(WIN)
    phase = (np.outer(index, index) % WIN) * (2.0 * np.pi / WIN)
    taper = np.sin((index + 0.5) * (np.pi / WIN)) / np.sqrt(WIN)
    cosine = np.cos(phase) * taper[None, :]
    sine = np.sin(phase) * taper[None, :]
    upper, lower = slice(0, STRIDE), slice(STRIDE, WIN)
    by_row = np.block(
        [
            [cosine[:, upper], sine[:, upper], cosine[:, lower], sine[:, lower]],
            [-sine[:, upper], cosine[:, upper], -sine[:, lower], cosine[:, lower]],
        ]
    )
    two = np.eye(2)
    by_col = np.block(
        [
            [np.kron(two, cosine.T), np.kron(two, -sine.T)],
            [np.kron(two, sine.T), np.kron(two, cosine.T)],
        ]
    )
    row_high, row_low = split_host(by_row)
    half = 2 * STRIDE
    col_high, col_low = split_host(by_col)
    return np.concatenate(
        [
            two_level(row_high[:, :half], row_low[:, :half], 256),
            two_level(row_high[:, half:], row_low[:, half:], 256),
            two_level(row_high, row_low, 256),
            two_level(row_high.T, row_low.T, 256),
            col_high, col_low,
        ],
        axis=0,
    )


def two_level(high, low, width):
    pad = np.zeros((high.shape[0], width - 2 * high.shape[1]), high.dtype)
    upper = np.concatenate([high, high, pad], axis=1)
    lower = np.concatenate([low, np.zeros_like(low), pad], axis=1)
    return np.concatenate([upper, lower], axis=0)


TABLE = host_tables()
OWN, NEXT, BOTH, BACK, COL_HIGH, COL_LOW = (slice(k * 256, (k + 1) * 256) for k in range(6))


def split(block):
    high = block.astype(BF16)
    return high, (block - high.astype(F32)).astype(BF16)


def mul(left, right):
    return jnp.dot(left, right, preferred_element_type=F32)


def by_rows(table, block):
    high, low = split(block)
    both = mul(table, jnp.concatenate([high, low], axis=0))
    return both[:128] + both[128:]


def turned(tiles):
    lane = lax.broadcasted_iota(jnp.int32, tiles[0].shape, 1)
    moved_tiles = [pltpu.roll(tile, STRIDE, axis=1) for tile in tiles]
    zero = jnp.zeros_like(tiles[0])
    return [
        jnp.where(lane < STRIDE, before, after)
        for before, after in zip([zero] + moved_tiles, moved_tiles + [zero])
    ]


def zero_kernel(out_ref):
    out_ref[...] = jnp.zeros_like(out_ref)


def zero_part():
    return pl.pallas_call(
        zero_kernel,
        out_shape=pltpu.VMEM((8, LANES), F32),
        out_specs=vmem(1)[0],
        compiler_params=pltpu.CompilerParams(vmem_limit_bytes=16 * 1024 * 1024),
        cost_estimate=pl.CostEstimate(flops=ZERO_FLOPS, bytes_accessed=4096, transcendentals=0),
        name="zero_part",
    )()


def first_kernel(holo_ref, zero_ref, out_ref):
    out_ref[...] = holo_ref[:, :LANES]


def first_part(holo, zero):
    return pl.pallas_call(
        first_kernel,
        out_shape=pltpu.VMEM((WIN, LANES), F32),
        in_specs=vmem(2),
        out_specs=vmem(1)[0],
        compiler_params=pltpu.CompilerParams(vmem_limit_bytes=16 * 1024 * 1024),
        cost_estimate=pl.CostEstimate(flops=0, bytes_accessed=4 * 10**5, transcendentals=0),
        name="first_part",
    )(holo, zero)


def local_kernel(holo_ref, target_ref, table_ref, levels_ref, partial_ref, energy_ref):
    pick = jnp.concatenate(picks(), axis=1)
    holo = holo_ref[...]
    energy = jnp.sum((holo * holo).reshape(8, 8, 1024), axis=0)
    energy_ref[...] = sum(energy[:, k * LANES:(k + 1) * LANES] for k in range(8))
    partial_ref[...] = by_rows(table_ref[OWN, :128], holo)
    lane = lax.broadcasted_iota(jnp.int32, (8, LANES), 1)
    row = lax.broadcasted_iota(jnp.int32, (8, LANES), 0)
    side = (row // 2) % 2
    here = (lane // WIN) == side
    same, other = [], []
    for kk in range(32):
        tile = target_ref[:, kk * LANES:(kk + 1) * LANES].astype(F32)
        turned = pltpu.roll(tile, WIN, axis=1)
        parts_same, parts_other = [], []
        for g in range(4):
            plain = tile[8 * g:8 * g + 8]
            moved = turned[8 * g:8 * g + 8]
            parts_same.append(jnp.where(here, jnp.where(side == 0, plain, moved), 0.0))
            parts_other.append(jnp.where(here, jnp.where(side == 0, moved, plain), 0.0))
        same.append(jnp.concatenate(parts_same, axis=1))
        other.append(jnp.concatenate(parts_other, axis=1))
    gathered = jnp.concatenate(same + other, axis=0).astype(BF16)
    placed = mul(pick, gathered)
    for g in range(4):
        for j2 in range(2):
            for e in range(2):
                start = (e * 8 + 2 * g + j2) * WIN
                source = (j2 * 2 + e) * WIN
                levels_ref[start:start + WIN, :] = placed[source:source + WIN, g * LANES:(g + 1) * LANES]


def along_cols(high, low, table_ref):
    table = jnp.concatenate([table_ref[COL_HIGH, :], table_ref[COL_HIGH, :], table_ref[COL_LOW, :]], axis=0)
    return mul(jnp.concatenate([high, low, high], axis=1), table)


def back_cols(high, low, table_ref):
    table = jnp.concatenate([table_ref[COL_HIGH, :], table_ref[COL_HIGH, :], table_ref[COL_LOW, :]], axis=1)
    fields = jnp.concatenate([high, low, high], axis=1)
    return lax.dot_general(fields, table, (((1,), (1,)), ((), ())), preferred_element_type=F32)


def picks():
    row = lax.broadcasted_iota(jnp.int32, (256, 256), 0)
    col = lax.broadcasted_iota(jnp.int32, (256, 256), 1)
    match = ((row >> 1) & 31) == (col >> 3)
    match = match & ((row >> 7) == ((col >> 2) & 1)) & (((row >> 6) & 1) == (col & 1))
    even = (row & 1) == 0
    return [jnp.where(match & side, 1.0, 0.0).astype(BF16) for side in (even, jnp.logical_not(even))]


def packed(*terms):
    sublane = lax.broadcasted_iota(jnp.int32, (8, LANES), 0)
    lane = lax.broadcasted_iota(jnp.int32, (8, LANES), 1)
    stack = jnp.zeros((8, LANES), F32)
    for k, term in enumerate(terms):
        stack = jnp.where(sublane == k, jnp.sum(term, axis=0, keepdims=True), stack)
    totals = jnp.sum(stack, axis=1, keepdims=True)
    return jnp.sum(jnp.where(lane == sublane, totals, 0.0), axis=0, keepdims=True)


def spread(fields, high_ref, low_ref, first):
    for j, field in enumerate(fields):
        at = slice((first + j) * WIN, (first + j + 1) * WIN)
        high, low = split(field)
        for c in range(2):
            to = slice(c * LANES, (c + 1) * LANES)
            high_ref[at, to] = high[c * WIN:(c + 1) * WIN]
            low_ref[at, to] = low[c * WIN:(c + 1) * WIN]


def back_by_stride(tiles):
    lane = lax.broadcasted_iota(jnp.int32, tiles[0].shape, 1)
    ahead = [pltpu.roll(tile, LANES - STRIDE, axis=1) for tile in tiles]
    return [jnp.where(lane < LANES - STRIDE, here, after) for here, after in zip(ahead[:-1], ahead[1:])]


def spectra(high_ref, low_ref, levels, table_ref, *terms):
    spectrum = along_cols(high_ref[...], low_ref[...], table_ref)
    real, imag = spectrum[:, :LANES], spectrum[:, LANES:]
    power = real * real + imag * imag
    return real, imag, power, packed(power * power, levels * power, *terms)


def adjoint_cols(real, imag, factor, table_ref):
    high, low = split(jnp.concatenate([real * factor, imag * factor], axis=1))
    return back_cols(high, low, table_ref)


def place(grid_ref, c, tile, at):
    high, low = split(tile)
    grid_ref[c * WIN:(c + 1) * WIN, at:at + LANES] = high
    grid_ref[128 + c * WIN:128 + (c + 1) * WIN, at:at + LANES] = low


def along_rows(grid, table_ref):
    result = mul(table_ref[BACK, :], grid)
    return result[:128] + result[128:]


def inner_kernel(
    below_ref, table_ref, levels_ref, partial_ref, energy_ref,
    grid_ref, last_ref, seam_ref, sums_ref,
    high_ref, low_ref,
):
    main = partial_ref[...] + by_rows(table_ref[NEXT, :128], below_ref[...])
    tiles = [main[:, j * LANES:(j + 1) * LANES] for j in range(8)]
    last_ref[...] = tiles[7]
    spread(tiles, high_ref, low_ref, 0)
    spread(back_by_stride(tiles), high_ref, low_ref, 8)
    levels = levels_ref[:INNER, :]
    real, imag, power, sums_ref[...] = spectra(high_ref, low_ref, levels, table_ref, energy_ref[...])
    for v, factor in enumerate((power, levels)):
        cols = adjoint_cols(real, imag, factor, table_ref)
        for c in range(2):
            lanes = slice(c * LANES, (c + 1) * LANES)
            odd = turned([cols[(8 + j) * WIN:(9 + j) * WIN, lanes] for j in range(7)])
            for j in range(7):
                place(grid_ref, c, odd[j] + cols[j * WIN:(j + 1) * WIN, lanes], (v * 7 + j) * LANES)
            seam_ref[v, c * WIN:(c + 1) * WIN] = odd[7] + cols[7 * WIN:8 * WIN, lanes]


def edge_kernel(
    right_ref, corner_ref, table_ref, levels_ref, grid_ref, last_ref, seam_ref, inner_sums_ref,
    own_ref, rows_ref, tail_ref, sums_hbm,
    high_ref, low_ref, edge_ref, copies_ref, fields_ref, sem,
):
    copy = pltpu.make_async_copy(copies_ref, sums_hbm, sem)
    levels = levels_ref[INNER:, :]

    @pl.when(pl.program_id(0) == 0)
    def _():
        edge = by_rows(table_ref[BOTH, :], jnp.concatenate([right_ref[...], corner_ref[...]], axis=0))
        spread(back_by_stride([last_ref[...], edge]), high_ref, low_ref, 0)
        real, imag, power, sums = spectra(high_ref, low_ref, levels, table_ref)
        fields_ref[0], fields_ref[1], fields_ref[2] = real, imag, power
        row = inner_sums_ref[...] + sums
        copies_ref[...] = jnp.broadcast_to(row[None], copies_ref.shape)
        copy.start()

    @pl.when(pl.program_id(0) == 1)
    def _():
        real, imag, power = fields_ref[0], fields_ref[1], fields_ref[2]
        for v, factor in enumerate((power, levels)):
            cols = adjoint_cols(real, imag, factor, table_ref)
            for c in range(2):
                seam, tail = turned([cols[:, c * LANES:(c + 1) * LANES]])
                place(edge_ref, c, seam + seam_ref[v, c * WIN:(c + 1) * WIN], v * 2 * LANES)
                place(edge_ref, c, tail, (v * 2 + 1) * LANES)
        result = along_rows(grid_ref[...], table_ref)
        for v in range(2):
            lanes = slice(v * 7 * LANES, (v + 1) * 7 * LANES)
            own_ref[v, :, :7 * LANES] = result[:WIN, lanes]
            rows_ref[v, :, :7 * LANES] = result[WIN:, lanes]
        result = along_rows(edge_ref[...], table_ref)
        for v in range(2):
            seam = result[:, v * 2 * LANES:(v * 2 + 1) * LANES]
            tail = result[:, (v * 2 + 1) * LANES:(v * 2 + 2) * LANES]
            own_ref[v, :, 7 * LANES:] = seam[:WIN]
            tail_ref[v] = tail[:WIN]
            rows_ref[v, :, 7 * LANES:8 * LANES] = seam[WIN:]
            rows_ref[v, :, 8 * LANES:] = tail[WIN:]
        copy.wait()


def vmem(count):
    return [pl.BlockSpec(memory_space=pltpu.VMEM)] * count


def local_part(*operands):
    return pl.pallas_call(
        local_kernel,
        out_shape=(
            pltpu.VMEM((1024, LANES), F32),
            pltpu.VMEM((128, 1024), F32),
            pltpu.VMEM((8, LANES), F32),
        ),
        in_specs=vmem(3),
        out_specs=tuple(vmem(3)),
        compiler_params=pltpu.CompilerParams(vmem_limit_bytes=24 * 1024 * 1024),
        cost_estimate=pl.CostEstimate(flops=10**8, bytes_accessed=3 * 10**6, transcendentals=0),
        name="local_part",
    )(*operands)


def inner_part(*operands):
    return pl.pallas_call(
        inner_kernel,
        out_shape=(
            pltpu.VMEM((256, 14 * LANES), BF16),
            pltpu.VMEM((128, LANES), F32),
            pltpu.VMEM((2, 128, LANES), F32),
            pltpu.VMEM((1, LANES), F32),
        ),
        in_specs=vmem(5),
        out_specs=tuple(vmem(4)),
        scratch_shapes=[
            pltpu.VMEM((INNER, 256), BF16),
            pltpu.VMEM((INNER, 256), BF16),
        ],
        compiler_params=pltpu.CompilerParams(vmem_limit_bytes=32 * 1024 * 1024),
        cost_estimate=pl.CostEstimate(flops=10**9, bytes_accessed=5 * 10**6, transcendentals=0),
        name="inner_part",
    )(*operands)


def edge_part(*operands):
    return pl.pallas_call(
        edge_kernel,
        out_shape=(
            pltpu.VMEM((2, WIN, 1024), F32),
            pltpu.VMEM((2, WIN, 1152), F32),
            pltpu.VMEM((2, WIN, LANES), F32),
            pltpu.HBM((32, 1, LANES), F32),
        ),
        grid=(2,),
        in_specs=vmem(8),
        out_specs=tuple(vmem(3)) + (pl.BlockSpec(memory_space=pl.ANY),),
        scratch_shapes=[
            pltpu.VMEM((WIN, 256), BF16),
            pltpu.VMEM((WIN, 256), BF16),
            pltpu.VMEM((256, 4 * LANES), BF16),
            pltpu.VMEM((32, 1, LANES), F32),
            pltpu.VMEM((3, WIN, LANES), F32),
            pltpu.SemaphoreType.DMA,
        ],
        compiler_params=pltpu.CompilerParams(vmem_limit_bytes=16 * 1024 * 1024),
        cost_estimate=pl.CostEstimate(flops=10**8, bytes_accessed=2 * 10**6, transcendentals=0),
        name="edge_part",
    )(*operands)


def merge_kernel(own_ref, rows_ref, both_ref):
    both_ref[...] = own_ref[...] + rows_ref[:, :, :1024]


def merge_part(*operands):
    return pl.pallas_call(
        merge_kernel,
        out_shape=pltpu.VMEM((2, WIN, 1024), F32),
        in_specs=vmem(2),
        out_specs=vmem(1)[0],
        compiler_params=pltpu.CompilerParams(vmem_limit_bytes=16 * 1024 * 1024),
        cost_estimate=pl.CostEstimate(flops=10**6, bytes_accessed=MERGE_BYTES, transcendentals=0),
        name="merge_part",
    )(*operands)


def combine_kernel(both_ref, cols_ref, holo_ref, sums_ref, out_hbm, out_ref, sems):
    total = jnp.sum(sums_ref[...], axis=0, keepdims=True)
    energy = total[:, 2:3] / CELLS + 1e-5
    moment = total[:, 0:1] / energy - total[:, 1:2]
    inverse = 1.0 / energy
    slope = moment / (energy * energy * CELLS)
    copies = []
    for k in range(4):
        at = slice(k * 16, (k + 1) * 16)
        out_ref[at, :] = both_ref[0, at] * inverse - both_ref[1, at] - slope * holo_ref[at, :]
        out_ref[at, :LANES] += cols_ref[0, at] * inverse - cols_ref[1, at]
        copy = pltpu.make_async_copy(out_ref.at[pl.ds(k * 16, 16)], out_hbm.at[pl.ds(k * 16, 16)], sems.at[k])
        copy.start()
        copies.append(copy)
    for copy in copies:
        copy.wait()


def combine(*operands):
    return pl.pallas_call(
        combine_kernel,
        out_shape=pltpu.HBM((WIN, 1024), F32),
        in_specs=vmem(4),
        out_specs=pl.BlockSpec(memory_space=pl.ANY),
        scratch_shapes=[pltpu.VMEM((WIN, 1024), F32), pltpu.SemaphoreType.DMA((4,))],
        compiler_params=pltpu.CompilerParams(vmem_limit_bytes=16 * 1024 * 1024),
        cost_estimate=pl.CostEstimate(flops=10**6, bytes_accessed=2 * 10**6, transcendentals=0),
        name="combine",
    )(*operands)


def moved(block, rows, cols):
    row_size, col_size = lax.axis_size("row"), lax.axis_size("col")
    route = [
        (r * col_size + c, (r + rows) * col_size + c + cols)
        for r in range(row_size)
        for c in range(col_size)
        if 0 <= r + rows < row_size and 0 <= c + cols < col_size
    ]
    return lax.ppermute(block, AXES, route)


def shared(values, bits):
    masks = [0]
    for bit in bits:
        masks = masks + [mask ^ (1 << bit) for mask in masks]
    every = masks[-1]
    order = [mask ^ (LEAD & every) for mask in masks]
    groups = [[base | mask for mask in order] for base in range(512) if base & every == 0]
    copies = values
    if copies.ndim == 2:
        copies = jnp.broadcast_to(values[None], (len(masks), 1, LANES))
    return lax.all_to_all(copies, AXES, 0, 0, axis_index_groups=groups, tiled=True)


def per_device(hologram, target):
    holo = hologram.reshape(WIN, 1024)
    below = moved(holo, -1, 0)
    first = first_part(holo, zero_part())
    corner = moved(first, -1, -1)
    right = moved(first, 0, -1)
    levels, partial, energy = local_part(holo, target.reshape(32, 4096), TABLE)
    inner = inner_part(below, TABLE, levels, partial, energy)
    own, rows, tail, sums = edge_part(right, corner, TABLE, levels, *inner)
    rows = moved(rows, 1, 0)
    cols = moved(tail + rows[:, :, 1024:], 0, 1)
    sums = jnp.sum(shared(sums, DEPTH_BITS), axis=0)
    both = merge_part(own, rows)
    both, sums = lax.optimization_barrier((both, sums))
    sums = shared(sums, PLANE_BITS).reshape(-1, LANES)
    return combine(both, cols, holo, sums).reshape(2, STRIDE, 1024)


def solution(mesh):
    return jax.shard_map(
        per_device,
        mesh=mesh,
        in_specs=(P(None, "row", "col"), P("row", "col", None)),
        out_specs=P(None, "row", "col"),
        check_vma=False,
    )
```

```python
import jax
import jax.numpy as jnp
import ml_dtypes
import numpy as np
from jax import lax
from jax.experimental import pallas as pl
from jax.experimental.pallas import tpu as pltpu
from jax.sharding import PartitionSpec as P

WIN = 64
STRIDE = WIN // 2
LANES = 128
AXES = ("row", "col")
DEPTH_BITS = (5, 1, 2, 3, 4)
PLANE_BITS = (0, 6, 7, 8)
LEAD = 11 * 32 + 20
BF16 = jnp.bfloat16
F32 = jnp.float32
CELLS = 512.0 * 32768.0
INNER = 15 * WIN
MERGE_BYTES = 300000
ZERO_FLOPS = 10**10


def split_host(table):
    high = table.astype(np.float32).astype(ml_dtypes.bfloat16)
    low = (table - high.astype(np.float64)).astype(np.float32).astype(ml_dtypes.bfloat16)
    return high, low


def host_tables():
    index = np.arange(WIN)
    phase = (np.outer(index, index) % WIN) * (2.0 * np.pi / WIN)
    taper = np.sin((index + 0.5) * (np.pi / WIN)) / np.sqrt(WIN)
    cosine = np.cos(phase) * taper[None, :]
    sine = np.sin(phase) * taper[None, :]
    upper, lower = slice(0, STRIDE), slice(STRIDE, WIN)
    by_row = np.block(
        [
            [cosine[:, upper], sine[:, upper], cosine[:, lower], sine[:, lower]],
            [-sine[:, upper], cosine[:, upper], -sine[:, lower], cosine[:, lower]],
        ]
    )
    two = np.eye(2)
    by_col = np.block(
        [
            [np.kron(two, cosine.T), np.kron(two, -sine.T)],
            [np.kron(two, sine.T), np.kron(two, cosine.T)],
        ]
    )
    row_high, row_low = split_host(by_row)
    half = 2 * STRIDE
    col_high, col_low = split_host(by_col)
    return np.concatenate(
        [
            two_level(row_high[:, :half], row_low[:, :half], 256),
            two_level(row_high[:, half:], row_low[:, half:], 256),
            two_level(row_high, row_low, 256),
            two_level(row_high.T, row_low.T, 256),
            col_high, col_low,
        ],
        axis=0,
    )


def two_level(high, low, width):
    pad = np.zeros((high.shape[0], width - 2 * high.shape[1]), high.dtype)
    upper = np.concatenate([high, high, pad], axis=1)
    lower = np.concatenate([low, np.zeros_like(low), pad], axis=1)
    return np.concatenate([upper, lower], axis=0)


TABLE = host_tables()
OWN, NEXT, BOTH, BACK, COL_HIGH, COL_LOW = (slice(k * 256, (k + 1) * 256) for k in range(6))


def split(block):
    high = block.astype(BF16)
    return high, (block - high.astype(F32)).astype(BF16)


def mul(left, right):
    return jnp.dot(left, right, preferred_element_type=F32)


def by_rows(table, block):
    high, low = split(block)
    both = mul(table, jnp.concatenate([high, low], axis=0))
    return both[:128] + both[128:]


def turned(tiles):
    lane = lax.broadcasted_iota(jnp.int32, tiles[0].shape, 1)
    moved_tiles = [pltpu.roll(tile, STRIDE, axis=1) for tile in tiles]
    zero = jnp.zeros_like(tiles[0])
    return [
        jnp.where(lane < STRIDE, before, after)
        for before, after in zip([zero] + moved_tiles, moved_tiles + [zero])
    ]


def zero_kernel(out_ref):
    out_ref[...] = jnp.zeros_like(out_ref)


def zero_part():
    return pl.pallas_call(
        zero_kernel,
        out_shape=pltpu.VMEM((8, LANES), F32),
        out_specs=vmem(1)[0],
        compiler_params=pltpu.CompilerParams(vmem_limit_bytes=16 * 1024 * 1024),
        cost_estimate=pl.CostEstimate(flops=ZERO_FLOPS, bytes_accessed=4096, transcendentals=0),
        name="zero_part",
    )()


def first_kernel(holo_ref, zero_ref, out_ref):
    out_ref[...] = holo_ref[:, :LANES]


def first_part(holo, zero):
    return pl.pallas_call(
        first_kernel,
        out_shape=pltpu.VMEM((WIN, LANES), F32),
        in_specs=vmem(2),
        out_specs=vmem(1)[0],
        compiler_params=pltpu.CompilerParams(vmem_limit_bytes=16 * 1024 * 1024),
        cost_estimate=pl.CostEstimate(flops=0, bytes_accessed=4 * 10**5, transcendentals=0),
        name="first_part",
    )(holo, zero)


def local_kernel(holo_ref, target_ref, table_ref, levels_ref, partial_ref, energy_ref):
    pick = jnp.concatenate(picks(), axis=1)
    holo = holo_ref[...]
    energy = jnp.sum((holo * holo).reshape(8, 8, 1024), axis=0)
    energy_ref[...] = sum(energy[:, k * LANES:(k + 1) * LANES] for k in range(8))
    partial_ref[...] = by_rows(table_ref[OWN, :128], holo)
    lane = lax.broadcasted_iota(jnp.int32, (8, LANES), 1)
    row = lax.broadcasted_iota(jnp.int32, (8, LANES), 0)
    side = (row // 2) % 2
    here = (lane // WIN) == side
    same, other = [], []
    for kk in range(32):
        tile = target_ref[:, kk * LANES:(kk + 1) * LANES].astype(F32)
        turned = pltpu.roll(tile, WIN, axis=1)
        parts_same, parts_other = [], []
        for g in range(4):
            plain = tile[8 * g:8 * g + 8]
            moved = turned[8 * g:8 * g + 8]
            parts_same.append(jnp.where(here, jnp.where(side == 0, plain, moved), 0.0))
            parts_other.append(jnp.where(here, jnp.where(side == 0, moved, plain), 0.0))
        same.append(jnp.concatenate(parts_same, axis=1))
        other.append(jnp.concatenate(parts_other, axis=1))
    gathered = jnp.concatenate(same + other, axis=0).astype(BF16)
    placed = mul(pick, gathered)
    for g in range(4):
        for j2 in range(2):
            for e in range(2):
                start = (e * 8 + 2 * g + j2) * WIN
                source = (j2 * 2 + e) * WIN
                levels_ref[start:start + WIN, :] = placed[source:source + WIN, g * LANES:(g + 1) * LANES]


def along_cols(high, low, table_ref):
    table = jnp.concatenate([table_ref[COL_HIGH, :], table_ref[COL_HIGH, :], table_ref[COL_LOW, :]], axis=0)
    return mul(jnp.concatenate([high, low, high], axis=1), table)


def back_cols(high, low, table_ref):
    table = jnp.concatenate([table_ref[COL_HIGH, :], table_ref[COL_HIGH, :], table_ref[COL_LOW, :]], axis=1)
    fields = jnp.concatenate([high, low, high], axis=1)
    return lax.dot_general(fields, table, (((1,), (1,)), ((), ())), preferred_element_type=F32)


def picks():
    row = lax.broadcasted_iota(jnp.int32, (256, 256), 0)
    col = lax.broadcasted_iota(jnp.int32, (256, 256), 1)
    match = ((row >> 1) & 31) == (col >> 3)
    match = match & ((row >> 7) == ((col >> 2) & 1)) & (((row >> 6) & 1) == (col & 1))
    even = (row & 1) == 0
    return [jnp.where(match & side, 1.0, 0.0).astype(BF16) for side in (even, jnp.logical_not(even))]


def packed(*terms):
    sublane = lax.broadcasted_iota(jnp.int32, (8, LANES), 0)
    lane = lax.broadcasted_iota(jnp.int32, (8, LANES), 1)
    stack = jnp.zeros((8, LANES), F32)
    for k, term in enumerate(terms):
        stack = jnp.where(sublane == k, jnp.sum(term, axis=0, keepdims=True), stack)
    totals = jnp.sum(stack, axis=1, keepdims=True)
    return jnp.sum(jnp.where(lane == sublane, totals, 0.0), axis=0, keepdims=True)


def spread(fields, high_ref, low_ref, first):
    for j, field in enumerate(fields):
        at = slice((first + j) * WIN, (first + j + 1) * WIN)
        high, low = split(field)
        for c in range(2):
            to = slice(c * LANES, (c + 1) * LANES)
            high_ref[at, to] = high[c * WIN:(c + 1) * WIN]
            low_ref[at, to] = low[c * WIN:(c + 1) * WIN]


def back_by_stride(tiles):
    lane = lax.broadcasted_iota(jnp.int32, tiles[0].shape, 1)
    ahead = [pltpu.roll(tile, LANES - STRIDE, axis=1) for tile in tiles]
    return [jnp.where(lane < LANES - STRIDE, here, after) for here, after in zip(ahead[:-1], ahead[1:])]


def spectra(high_ref, low_ref, levels, table_ref, *terms):
    spectrum = along_cols(high_ref[...], low_ref[...], table_ref)
    real, imag = spectrum[:, :LANES], spectrum[:, LANES:]
    power = real * real + imag * imag
    return real, imag, power, packed(power * power, levels * power, *terms)


def adjoint_cols(real, imag, factor, table_ref):
    high, low = split(jnp.concatenate([real * factor, imag * factor], axis=1))
    return back_cols(high, low, table_ref)


def place(grid_ref, c, tile, at):
    high, low = split(tile)
    grid_ref[c * WIN:(c + 1) * WIN, at:at + LANES] = high
    grid_ref[128 + c * WIN:128 + (c + 1) * WIN, at:at + LANES] = low


def along_rows(grid, table_ref):
    result = mul(table_ref[BACK, :], grid)
    return result[:128] + result[128:]


def inner_kernel(
    below_ref, table_ref, levels_ref, partial_ref, energy_ref,
    grid_ref, last_ref, seam_ref, sums_ref,
    high_ref, low_ref,
):
    main = partial_ref[...] + by_rows(table_ref[NEXT, :128], below_ref[...])
    tiles = [main[:, j * LANES:(j + 1) * LANES] for j in range(8)]
    last_ref[...] = tiles[7]
    spread(tiles, high_ref, low_ref, 0)
    spread(back_by_stride(tiles), high_ref, low_ref, 8)
    levels = levels_ref[:INNER, :]
    real, imag, power, sums_ref[...] = spectra(high_ref, low_ref, levels, table_ref, energy_ref[...])
    for v, factor in enumerate((power, levels)):
        cols = adjoint_cols(real, imag, factor, table_ref)
        for c in range(2):
            lanes = slice(c * LANES, (c + 1) * LANES)
            odd = turned([cols[(8 + j) * WIN:(9 + j) * WIN, lanes] for j in range(7)])
            for j in range(7):
                place(grid_ref, c, odd[j] + cols[j * WIN:(j + 1) * WIN, lanes], (v * 7 + j) * LANES)
            seam_ref[v, c * WIN:(c + 1) * WIN] = odd[7] + cols[7 * WIN:8 * WIN, lanes]


def folded(product):
    half = product.shape[0] // 2
    return product[:half, :256] + product[half:, :256] + product[:half, 256:]


def edge_kernel(
    right_ref, corner_ref, table_ref, levels_ref, grid_ref, last_ref, seam_ref, inner_sums_ref,
    own_ref, rows_ref, tail_ref, sums_hbm,
    high_ref, low_ref, edge_ref, copies_ref, fields_ref, sem,
):
    copy = pltpu.make_async_copy(copies_ref, sums_hbm, sem)
    levels = levels_ref[INNER:, :]

    @pl.when(pl.program_id(0) == 0)
    def _():
        edge = by_rows(table_ref[BOTH, :], jnp.concatenate([right_ref[...], corner_ref[...]], axis=0))
        spread(back_by_stride([last_ref[...], edge]), high_ref, low_ref, 0)
        fields = jnp.concatenate([high_ref[...], low_ref[...]], axis=0)
        table = jnp.concatenate([table_ref[COL_HIGH, :], table_ref[COL_LOW, :]], axis=1)
        spectrum = folded(mul(fields, table))
        real, imag = spectrum[:, :LANES], spectrum[:, LANES:]
        power = real * real + imag * imag
        sums = packed(power * power, levels * power)
        fields_ref[0], fields_ref[1], fields_ref[2] = real, imag, power
        row = inner_sums_ref[...] + sums
        copies_ref[...] = jnp.broadcast_to(row[None], copies_ref.shape)
        copy.start()

    @pl.when(pl.program_id(0) == 1)
    def _():
        real, imag, power = fields_ref[0], fields_ref[1], fields_ref[2]
        weighted = [jnp.concatenate([real * factor, imag * factor], axis=1) for factor in (power, levels)]
        fields = jnp.concatenate(split(jnp.concatenate(weighted, axis=0)), axis=0)
        table = jnp.concatenate([table_ref[COL_HIGH, :], table_ref[COL_LOW, :]], axis=0)
        both = folded(lax.dot_general(fields, table, (((1,), (1,)), ((), ())), preferred_element_type=F32))
        for v in range(2):
            cols = both[v * WIN:(v + 1) * WIN]
            for c in range(2):
                seam, tail = turned([cols[:, c * LANES:(c + 1) * LANES]])
                place(edge_ref, c, seam + seam_ref[v, c * WIN:(c + 1) * WIN], v * 2 * LANES)
                place(edge_ref, c, tail, (v * 2 + 1) * LANES)
        result = along_rows(grid_ref[...], table_ref)
        for v in range(2):
            lanes = slice(v * 7 * LANES, (v + 1) * 7 * LANES)
            own_ref[v, :, :7 * LANES] = result[:WIN, lanes]
            rows_ref[v, :, :7 * LANES] = result[WIN:, lanes]
        result = along_rows(edge_ref[...], table_ref)
        for v in range(2):
            seam = result[:, v * 2 * LANES:(v * 2 + 1) * LANES]
            tail = result[:, (v * 2 + 1) * LANES:(v * 2 + 2) * LANES]
            own_ref[v, :, 7 * LANES:] = seam[:WIN]
            tail_ref[v] = tail[:WIN]
            rows_ref[v, :, 7 * LANES:8 * LANES] = seam[WIN:]
            rows_ref[v, :, 8 * LANES:] = tail[WIN:]
        copy.wait()


def vmem(count):
    return [pl.BlockSpec(memory_space=pltpu.VMEM)] * count


def local_part(*operands):
    return pl.pallas_call(
        local_kernel,
        out_shape=(
            pltpu.VMEM((1024, LANES), F32),
            pltpu.VMEM((128, 1024), F32),
            pltpu.VMEM((8, LANES), F32),
        ),
        in_specs=vmem(3),
        out_specs=tuple(vmem(3)),
        compiler_params=pltpu.CompilerParams(vmem_limit_bytes=24 * 1024 * 1024),
        cost_estimate=pl.CostEstimate(flops=10**8, bytes_accessed=3 * 10**6, transcendentals=0),
        name="local_part",
    )(*operands)


def inner_part(*operands):
    return pl.pallas_call(
        inner_kernel,
        out_shape=(
            pltpu.VMEM((256, 14 * LANES), BF16),
            pltpu.VMEM((128, LANES), F32),
            pltpu.VMEM((2, 128, LANES), F32),
            pltpu.VMEM((1, LANES), F32),
        ),
        in_specs=vmem(5),
        out_specs=tuple(vmem(4)),
        scratch_shapes=[
            pltpu.VMEM((INNER, 256), BF16),
            pltpu.VMEM((INNER, 256), BF16),
        ],
        compiler_params=pltpu.CompilerParams(vmem_limit_bytes=32 * 1024 * 1024),
        cost_estimate=pl.CostEstimate(flops=10**9, bytes_accessed=5 * 10**6, transcendentals=0),
        name="inner_part",
    )(*operands)


def edge_part(*operands):
    return pl.pallas_call(
        edge_kernel,
        out_shape=(
            pltpu.VMEM((2, WIN, 1024), F32),
            pltpu.VMEM((2, WIN, 1152), F32),
            pltpu.VMEM((2, WIN, LANES), F32),
            pltpu.HBM((32, 1, LANES), F32),
        ),
        grid=(2,),
        in_specs=vmem(8),
        out_specs=tuple(vmem(3)) + (pl.BlockSpec(memory_space=pl.ANY),),
        scratch_shapes=[
            pltpu.VMEM((WIN, 256), BF16),
            pltpu.VMEM((WIN, 256), BF16),
            pltpu.VMEM((256, 4 * LANES), BF16),
            pltpu.VMEM((32, 1, LANES), F32),
            pltpu.VMEM((3, WIN, LANES), F32),
            pltpu.SemaphoreType.DMA,
        ],
        compiler_params=pltpu.CompilerParams(vmem_limit_bytes=16 * 1024 * 1024),
        cost_estimate=pl.CostEstimate(flops=10**8, bytes_accessed=2 * 10**6, transcendentals=0),
        name="edge_part",
    )(*operands)


def merge_kernel(own_ref, rows_ref, both_ref):
    both_ref[...] = own_ref[...] + rows_ref[:, :, :1024]


def merge_part(*operands):
    return pl.pallas_call(
        merge_kernel,
        out_shape=pltpu.VMEM((2, WIN, 1024), F32),
        in_specs=vmem(2),
        out_specs=vmem(1)[0],
        compiler_params=pltpu.CompilerParams(vmem_limit_bytes=16 * 1024 * 1024),
        cost_estimate=pl.CostEstimate(flops=10**6, bytes_accessed=MERGE_BYTES, transcendentals=0),
        name="merge_part",
    )(*operands)


def combine_kernel(both_ref, cols_ref, holo_ref, sums_ref, out_hbm, out_ref, sems):
    total = jnp.sum(sums_ref[...], axis=0, keepdims=True)
    energy = total[:, 2:3] / CELLS + 1e-5
    moment = total[:, 0:1] / energy - total[:, 1:2]
    inverse = 1.0 / energy
    slope = moment / (energy * energy * CELLS)
    copies = []
    for k in range(4):
        at = slice(k * 16, (k + 1) * 16)
        out_ref[at, :] = both_ref[0, at] * inverse - both_ref[1, at] - slope * holo_ref[at, :]
        out_ref[at, :LANES] += cols_ref[0, at] * inverse - cols_ref[1, at]
        copy = pltpu.make_async_copy(out_ref.at[pl.ds(k * 16, 16)], out_hbm.at[pl.ds(k * 16, 16)], sems.at[k])
        copy.start()
        copies.append(copy)
    for copy in copies:
        copy.wait()


def combine(*operands):
    return pl.pallas_call(
        combine_kernel,
        out_shape=pltpu.HBM((WIN, 1024), F32),
        in_specs=vmem(4),
        out_specs=pl.BlockSpec(memory_space=pl.ANY),
        scratch_shapes=[pltpu.VMEM((WIN, 1024), F32), pltpu.SemaphoreType.DMA((4,))],
        compiler_params=pltpu.CompilerParams(vmem_limit_bytes=16 * 1024 * 1024),
        cost_estimate=pl.CostEstimate(flops=10**6, bytes_accessed=2 * 10**6, transcendentals=0),
        name="combine",
    )(*operands)


def moved(block, rows, cols):
    row_size, col_size = lax.axis_size("row"), lax.axis_size("col")
    route = [
        (r * col_size + c, (r + rows) * col_size + c + cols)
        for r in range(row_size)
        for c in range(col_size)
        if 0 <= r + rows < row_size and 0 <= c + cols < col_size
    ]
    return lax.ppermute(block, AXES, route)


def shared(values, bits):
    masks = [0]
    for bit in bits:
        masks = masks + [mask ^ (1 << bit) for mask in masks]
    every = masks[-1]
    order = [mask ^ (LEAD & every) for mask in masks]
    groups = [[base | mask for mask in order] for base in range(512) if base & every == 0]
    copies = values
    if copies.ndim == 2:
        copies = jnp.broadcast_to(values[None], (len(masks), 1, LANES))
    return lax.all_to_all(copies, AXES, 0, 0, axis_index_groups=groups, tiled=True)


def per_device(hologram, target):
    holo = hologram.reshape(WIN, 1024)
    below = moved(holo, -1, 0)
    first = first_part(holo, zero_part())
    corner = moved(first, -1, -1)
    right = moved(first, 0, -1)
    levels, partial, energy = local_part(holo, target.reshape(32, 4096), TABLE)
    inner = inner_part(below, TABLE, levels, partial, energy)
    own, rows, tail, sums = edge_part(right, corner, TABLE, levels, *inner)
    rows = moved(rows, 1, 0)
    cols = moved(tail + rows[:, :, 1024:], 0, 1)
    sums = jnp.sum(shared(sums, DEPTH_BITS), axis=0)
    both = merge_part(own, rows)
    both, sums = lax.optimization_barrier((both, sums))
    sums = shared(sums, PLANE_BITS).reshape(-1, LANES)
    return combine(both, cols, holo, sums).reshape(2, STRIDE, 1024)


def solution(mesh):
    return jax.shard_map(
        per_device,
        mesh=mesh,
        in_specs=(P(None, "row", "col"), P("row", "col", None)),
        out_specs=P(None, "row", "col"),
        check_vma=False,
    )
```

```python
import jax
import jax.numpy as jnp
import ml_dtypes
import numpy as np
from jax import lax
from jax.experimental import pallas as pl
from jax.experimental.pallas import tpu as pltpu
from jax.sharding import PartitionSpec as P

WIN = 64
STRIDE = WIN // 2
LANES = 128
AXES = ("row", "col")
DEPTH_BITS = (5, 1, 2, 3, 4)
PLANE_BITS = (0, 6, 7, 8)
LEAD = 11 * 32 + 20
BF16 = jnp.bfloat16
F32 = jnp.float32
CELLS = 512.0 * 32768.0
INNER = 15 * WIN
MERGE_BYTES = 300000
ZERO_FLOPS = 10**10


def split_host(table):
    high = table.astype(np.float32).astype(ml_dtypes.bfloat16)
    low = (table - high.astype(np.float64)).astype(np.float32).astype(ml_dtypes.bfloat16)
    return high, low


def host_tables():
    index = np.arange(WIN)
    phase = (np.outer(index, index) % WIN) * (2.0 * np.pi / WIN)
    taper = np.sin((index + 0.5) * (np.pi / WIN)) / np.sqrt(WIN)
    cosine = np.cos(phase) * taper[None, :]
    sine = np.sin(phase) * taper[None, :]
    upper, lower = slice(0, STRIDE), slice(STRIDE, WIN)
    by_row = np.block(
        [
            [cosine[:, upper], sine[:, upper], cosine[:, lower], sine[:, lower]],
            [-sine[:, upper], cosine[:, upper], -sine[:, lower], cosine[:, lower]],
        ]
    )
    two = np.eye(2)
    by_col = np.block(
        [
            [np.kron(two, cosine.T), np.kron(two, -sine.T)],
            [np.kron(two, sine.T), np.kron(two, cosine.T)],
        ]
    )
    row_high, row_low = split_host(by_row)
    half = 2 * STRIDE
    col_high, col_low = split_host(by_col)
    return np.concatenate(
        [
            two_level(row_high[:, :half], row_low[:, :half], 256),
            two_level(row_high[:, half:], row_low[:, half:], 256),
            two_level(row_high, row_low, 256),
            two_level(row_high.T, row_low.T, 256),
            col_high, col_low,
        ],
        axis=0,
    )


def two_level(high, low, width):
    pad = np.zeros((high.shape[0], width - 2 * high.shape[1]), high.dtype)
    upper = np.concatenate([high, high, pad], axis=1)
    lower = np.concatenate([low, np.zeros_like(low), pad], axis=1)
    return np.concatenate([upper, lower], axis=0)


TABLE = host_tables()
OWN, NEXT, BOTH, BACK, COL_HIGH, COL_LOW = (slice(k * 256, (k + 1) * 256) for k in range(6))


def split(block):
    high = block.astype(BF16)
    return high, (block - high.astype(F32)).astype(BF16)


def mul(left, right):
    return jnp.dot(left, right, preferred_element_type=F32)


def by_rows(table, block):
    high, low = split(block)
    both = mul(table, jnp.concatenate([high, low], axis=0))
    return both[:128] + both[128:]


def turned(tiles):
    lane = lax.broadcasted_iota(jnp.int32, tiles[0].shape, 1)
    moved_tiles = [pltpu.roll(tile, STRIDE, axis=1) for tile in tiles]
    zero = jnp.zeros_like(tiles[0])
    return [
        jnp.where(lane < STRIDE, before, after)
        for before, after in zip([zero] + moved_tiles, moved_tiles + [zero])
    ]


def zero_kernel(out_ref):
    out_ref[...] = jnp.zeros_like(out_ref)


def zero_part():
    return pl.pallas_call(
        zero_kernel,
        out_shape=pltpu.VMEM((8, LANES), F32),
        out_specs=vmem(1)[0],
        compiler_params=pltpu.CompilerParams(vmem_limit_bytes=16 * 1024 * 1024),
        cost_estimate=pl.CostEstimate(flops=ZERO_FLOPS, bytes_accessed=4096, transcendentals=0),
        name="zero_part",
    )()


def first_kernel(holo_ref, zero_ref, out_ref):
    out_ref[...] = holo_ref[:, :LANES]


def first_part(holo, zero):
    return pl.pallas_call(
        first_kernel,
        out_shape=pltpu.VMEM((WIN, LANES), F32),
        in_specs=vmem(2),
        out_specs=vmem(1)[0],
        compiler_params=pltpu.CompilerParams(vmem_limit_bytes=16 * 1024 * 1024),
        cost_estimate=pl.CostEstimate(flops=0, bytes_accessed=4 * 10**5, transcendentals=0),
        name="first_part",
    )(holo, zero)


def local_kernel(holo_ref, target_ref, table_ref, levels_ref, partial_ref, energy_ref):
    pick = jnp.concatenate(picks(), axis=1)
    holo = holo_ref[...]
    energy = jnp.sum((holo * holo).reshape(8, 8, 1024), axis=0)
    energy_ref[...] = sum(energy[:, k * LANES:(k + 1) * LANES] for k in range(8))
    partial_ref[...] = by_rows(table_ref[OWN, :128], holo)
    lane = lax.broadcasted_iota(jnp.int32, (8, LANES), 1)
    row = lax.broadcasted_iota(jnp.int32, (8, LANES), 0)
    side = (row // 2) % 2
    here = (lane // WIN) == side
    same, other = [], []
    for kk in range(32):
        tile = target_ref[:, kk * LANES:(kk + 1) * LANES].astype(F32)
        turned = pltpu.roll(tile, WIN, axis=1)
        parts_same, parts_other = [], []
        for g in range(4):
            plain = tile[8 * g:8 * g + 8]
            moved = turned[8 * g:8 * g + 8]
            parts_same.append(jnp.where(here, jnp.where(side == 0, plain, moved), 0.0))
            parts_other.append(jnp.where(here, jnp.where(side == 0, moved, plain), 0.0))
        same.append(jnp.concatenate(parts_same, axis=1))
        other.append(jnp.concatenate(parts_other, axis=1))
    gathered = jnp.concatenate(same + other, axis=0).astype(BF16)
    placed = mul(pick, gathered)
    for g in range(4):
        for j2 in range(2):
            for e in range(2):
                start = (e * 8 + 2 * g + j2) * WIN
                source = (j2 * 2 + e) * WIN
                levels_ref[start:start + WIN, :] = placed[source:source + WIN, g * LANES:(g + 1) * LANES]


def along_cols(high, low, table_ref):
    table = jnp.concatenate([table_ref[COL_HIGH, :], table_ref[COL_HIGH, :], table_ref[COL_LOW, :]], axis=0)
    return mul(jnp.concatenate([high, low, high], axis=1), table)


def back_cols(high, low, table_ref):
    table = jnp.concatenate([table_ref[COL_HIGH, :], table_ref[COL_HIGH, :], table_ref[COL_LOW, :]], axis=1)
    fields = jnp.concatenate([high, low, high], axis=1)
    return lax.dot_general(fields, table, (((1,), (1,)), ((), ())), preferred_element_type=F32)


def picks():
    row = lax.broadcasted_iota(jnp.int32, (256, 256), 0)
    col = lax.broadcasted_iota(jnp.int32, (256, 256), 1)
    match = ((row >> 1) & 31) == (col >> 3)
    match = match & ((row >> 7) == ((col >> 2) & 1)) & (((row >> 6) & 1) == (col & 1))
    even = (row & 1) == 0
    return [jnp.where(match & side, 1.0, 0.0).astype(BF16) for side in (even, jnp.logical_not(even))]


def packed(*terms):
    sublane = lax.broadcasted_iota(jnp.int32, (8, LANES), 0)
    lane = lax.broadcasted_iota(jnp.int32, (8, LANES), 1)
    stack = jnp.zeros((8, LANES), F32)
    for k, term in enumerate(terms):
        stack = jnp.where(sublane == k, jnp.sum(term, axis=0, keepdims=True), stack)
    totals = jnp.sum(stack, axis=1, keepdims=True)
    return jnp.sum(jnp.where(lane == sublane, totals, 0.0), axis=0, keepdims=True)


def spread(fields, high_ref, low_ref, first):
    for j, field in enumerate(fields):
        at = slice((first + j) * WIN, (first + j + 1) * WIN)
        high, low = split(field)
        for c in range(2):
            to = slice(c * LANES, (c + 1) * LANES)
            high_ref[at, to] = high[c * WIN:(c + 1) * WIN]
            low_ref[at, to] = low[c * WIN:(c + 1) * WIN]


def back_by_stride(tiles):
    lane = lax.broadcasted_iota(jnp.int32, tiles[0].shape, 1)
    ahead = [pltpu.roll(tile, LANES - STRIDE, axis=1) for tile in tiles]
    return [jnp.where(lane < LANES - STRIDE, here, after) for here, after in zip(ahead[:-1], ahead[1:])]


def spectra(high_ref, low_ref, levels, table_ref, *terms):
    spectrum = along_cols(high_ref[...], low_ref[...], table_ref)
    real, imag = spectrum[:, :LANES], spectrum[:, LANES:]
    power = real * real + imag * imag
    return real, imag, power, packed(power * power, levels * power, *terms)


def adjoint_cols(real, imag, factor, table_ref):
    high, low = split(jnp.concatenate([real * factor, imag * factor], axis=1))
    return back_cols(high, low, table_ref)


def place(grid_ref, c, tile, at):
    high, low = split(tile)
    grid_ref[c * WIN:(c + 1) * WIN, at:at + LANES] = high
    grid_ref[128 + c * WIN:128 + (c + 1) * WIN, at:at + LANES] = low


def along_rows(grid, table_ref):
    result = mul(table_ref[BACK, :], grid)
    return result[:128] + result[128:]


def inner_kernel(
    below_ref, table_ref, levels_ref, partial_ref, energy_ref,
    grid_ref, last_ref, seam_ref, sums_ref,
    high_ref, low_ref,
):
    main = partial_ref[...] + by_rows(table_ref[NEXT, :128], below_ref[...])
    tiles = [main[:, j * LANES:(j + 1) * LANES] for j in range(8)]
    last_ref[...] = tiles[7]
    spread(tiles, high_ref, low_ref, 0)
    spread(back_by_stride(tiles), high_ref, low_ref, 8)
    levels = levels_ref[:INNER, :]
    real, imag, power, sums_ref[...] = spectra(high_ref, low_ref, levels, table_ref, energy_ref[...])
    for v, factor in enumerate((power, levels)):
        cols = adjoint_cols(real, imag, factor, table_ref)
        for c in range(2):
            lanes = slice(c * LANES, (c + 1) * LANES)
            odd = turned([cols[(8 + j) * WIN:(9 + j) * WIN, lanes] for j in range(7)])
            for j in range(7):
                place(grid_ref, c, odd[j] + cols[j * WIN:(j + 1) * WIN, lanes], (v * 7 + j) * LANES)
            seam_ref[v, c * WIN:(c + 1) * WIN] = odd[7] + cols[7 * WIN:8 * WIN, lanes]


def folded(product):
    half = product.shape[0] // 2
    return product[:half, :256] + product[half:, :256] + product[:half, 256:]


def edge_kernel(
    right_ref, corner_ref, table_ref, levels_ref, grid_ref, last_ref, seam_ref, inner_sums_ref,
    own_ref, rows_ref, tail_ref, sums_hbm,
    high_ref, low_ref, edge_ref, copies_ref, fields_ref, sem,
):
    copy = pltpu.make_async_copy(copies_ref, sums_hbm, sem)
    levels = levels_ref[INNER:, :]

    @pl.when(pl.program_id(0) == 0)
    def _():
        edge = by_rows(table_ref[BOTH, :], jnp.concatenate([right_ref[...], corner_ref[...]], axis=0))
        pair = [jnp.concatenate([part[:WIN], part[WIN:]], axis=1) for part in split(back_by_stride([last_ref[...], edge])[0])]
        fields = jnp.concatenate(pair, axis=0)
        table = jnp.concatenate([table_ref[COL_HIGH, :], table_ref[COL_LOW, :]], axis=1)
        spectrum = folded(mul(fields, table))
        real, imag = spectrum[:, :LANES], spectrum[:, LANES:]
        power = real * real + imag * imag
        sums = packed(power * power, levels * power)
        fields_ref[0], fields_ref[1], fields_ref[2] = real, imag, power
        row = inner_sums_ref[...] + sums
        copies_ref[...] = jnp.broadcast_to(row[None], copies_ref.shape)
        copy.start()

    @pl.when(pl.program_id(0) == 1)
    def _():
        real, imag, power = fields_ref[0], fields_ref[1], fields_ref[2]
        weighted = [jnp.concatenate([real * factor, imag * factor], axis=1) for factor in (power, levels)]
        fields = jnp.concatenate(split(jnp.concatenate(weighted, axis=0)), axis=0)
        table = jnp.concatenate([table_ref[COL_HIGH, :], table_ref[COL_LOW, :]], axis=0)
        both = folded(lax.dot_general(fields, table, (((1,), (1,)), ((), ())), preferred_element_type=F32))
        for v in range(2):
            cols = both[v * WIN:(v + 1) * WIN]
            for c in range(2):
                seam, tail = turned([cols[:, c * LANES:(c + 1) * LANES]])
                place(edge_ref, c, seam + seam_ref[v, c * WIN:(c + 1) * WIN], v * 2 * LANES)
                place(edge_ref, c, tail, (v * 2 + 1) * LANES)
        result = along_rows(grid_ref[...], table_ref)
        for v in range(2):
            lanes = slice(v * 7 * LANES, (v + 1) * 7 * LANES)
            own_ref[v, :, :7 * LANES] = result[:WIN, lanes]
            rows_ref[v, :, :7 * LANES] = result[WIN:, lanes]
        result = along_rows(edge_ref[...], table_ref)
        for v in range(2):
            seam = result[:, v * 2 * LANES:(v * 2 + 1) * LANES]
            tail = result[:, (v * 2 + 1) * LANES:(v * 2 + 2) * LANES]
            own_ref[v, :, 7 * LANES:] = seam[:WIN]
            tail_ref[v] = tail[:WIN]
            rows_ref[v, :, 7 * LANES:8 * LANES] = seam[WIN:]
            rows_ref[v, :, 8 * LANES:] = tail[WIN:]
        copy.wait()


def vmem(count):
    return [pl.BlockSpec(memory_space=pltpu.VMEM)] * count


def local_part(*operands):
    return pl.pallas_call(
        local_kernel,
        out_shape=(
            pltpu.VMEM((1024, LANES), F32),
            pltpu.VMEM((128, 1024), F32),
            pltpu.VMEM((8, LANES), F32),
        ),
        in_specs=vmem(3),
        out_specs=tuple(vmem(3)),
        compiler_params=pltpu.CompilerParams(vmem_limit_bytes=24 * 1024 * 1024),
        cost_estimate=pl.CostEstimate(flops=10**8, bytes_accessed=3 * 10**6, transcendentals=0),
        name="local_part",
    )(*operands)


def inner_part(*operands):
    return pl.pallas_call(
        inner_kernel,
        out_shape=(
            pltpu.VMEM((256, 14 * LANES), BF16),
            pltpu.VMEM((128, LANES), F32),
            pltpu.VMEM((2, 128, LANES), F32),
            pltpu.VMEM((1, LANES), F32),
        ),
        in_specs=vmem(5),
        out_specs=tuple(vmem(4)),
        scratch_shapes=[
            pltpu.VMEM((INNER, 256), BF16),
            pltpu.VMEM((INNER, 256), BF16),
        ],
        compiler_params=pltpu.CompilerParams(vmem_limit_bytes=32 * 1024 * 1024),
        cost_estimate=pl.CostEstimate(flops=10**9, bytes_accessed=5 * 10**6, transcendentals=0),
        name="inner_part",
    )(*operands)


def edge_part(*operands):
    return pl.pallas_call(
        edge_kernel,
        out_shape=(
            pltpu.VMEM((2, WIN, 1024), F32),
            pltpu.VMEM((2, WIN, 1152), F32),
            pltpu.VMEM((2, WIN, LANES), F32),
            pltpu.HBM((32, 1, LANES), F32),
        ),
        grid=(2,),
        in_specs=vmem(8),
        out_specs=tuple(vmem(3)) + (pl.BlockSpec(memory_space=pl.ANY),),
        scratch_shapes=[
            pltpu.VMEM((WIN, 256), BF16),
            pltpu.VMEM((WIN, 256), BF16),
            pltpu.VMEM((256, 4 * LANES), BF16),
            pltpu.VMEM((32, 1, LANES), F32),
            pltpu.VMEM((3, WIN, LANES), F32),
            pltpu.SemaphoreType.DMA,
        ],
        compiler_params=pltpu.CompilerParams(vmem_limit_bytes=16 * 1024 * 1024),
        cost_estimate=pl.CostEstimate(flops=10**8, bytes_accessed=2 * 10**6, transcendentals=0),
        name="edge_part",
    )(*operands)


def merge_kernel(own_ref, rows_ref, both_ref):
    both_ref[...] = own_ref[...] + rows_ref[:, :, :1024]


def merge_part(*operands):
    return pl.pallas_call(
        merge_kernel,
        out_shape=pltpu.VMEM((2, WIN, 1024), F32),
        in_specs=vmem(2),
        out_specs=vmem(1)[0],
        compiler_params=pltpu.CompilerParams(vmem_limit_bytes=16 * 1024 * 1024),
        cost_estimate=pl.CostEstimate(flops=10**6, bytes_accessed=MERGE_BYTES, transcendentals=0),
        name="merge_part",
    )(*operands)


def combine_kernel(both_ref, cols_ref, holo_ref, sums_ref, out_hbm, out_ref, sems):
    total = jnp.sum(sums_ref[...], axis=0, keepdims=True)
    energy = total[:, 2:3] / CELLS + 1e-5
    moment = total[:, 0:1] / energy - total[:, 1:2]
    inverse = 1.0 / energy
    slope = moment / (energy * energy * CELLS)
    copies = []
    for k in range(4):
        at = slice(k * 16, (k + 1) * 16)
        out_ref[at, :] = both_ref[0, at] * inverse - both_ref[1, at] - slope * holo_ref[at, :]
        out_ref[at, :LANES] += cols_ref[0, at] * inverse - cols_ref[1, at]
        copy = pltpu.make_async_copy(out_ref.at[pl.ds(k * 16, 16)], out_hbm.at[pl.ds(k * 16, 16)], sems.at[k])
        copy.start()
        copies.append(copy)
    for copy in copies:
        copy.wait()


def combine(*operands):
    return pl.pallas_call(
        combine_kernel,
        out_shape=pltpu.HBM((WIN, 1024), F32),
        in_specs=vmem(4),
        out_specs=pl.BlockSpec(memory_space=pl.ANY),
        scratch_shapes=[pltpu.VMEM((WIN, 1024), F32), pltpu.SemaphoreType.DMA((4,))],
        compiler_params=pltpu.CompilerParams(vmem_limit_bytes=16 * 1024 * 1024),
        cost_estimate=pl.CostEstimate(flops=10**6, bytes_accessed=2 * 10**6, transcendentals=0),
        name="combine",
    )(*operands)


def moved(block, rows, cols):
    row_size, col_size = lax.axis_size("row"), lax.axis_size("col")
    route = [
        (r * col_size + c, (r + rows) * col_size + c + cols)
        for r in range(row_size)
        for c in range(col_size)
        if 0 <= r + rows < row_size and 0 <= c + cols < col_size
    ]
    return lax.ppermute(block, AXES, route)


def shared(values, bits):
    masks = [0]
    for bit in bits:
        masks = masks + [mask ^ (1 << bit) for mask in masks]
    every = masks[-1]
    order = [mask ^ (LEAD & every) for mask in masks]
    groups = [[base | mask for mask in order] for base in range(512) if base & every == 0]
    copies = values
    if copies.ndim == 2:
        copies = jnp.broadcast_to(values[None], (len(masks), 1, LANES))
    return lax.all_to_all(copies, AXES, 0, 0, axis_index_groups=groups, tiled=True)


def per_device(hologram, target):
    holo = hologram.reshape(WIN, 1024)
    below = moved(holo, -1, 0)
    first = first_part(holo, zero_part())
    corner = moved(first, -1, -1)
    right = moved(first, 0, -1)
    levels, partial, energy = local_part(holo, target.reshape(32, 4096), TABLE)
    inner = inner_part(below, TABLE, levels, partial, energy)
    own, rows, tail, sums = edge_part(right, corner, TABLE, levels, *inner)
    rows = moved(rows, 1, 0)
    cols = moved(tail + rows[:, :, 1024:], 0, 1)
    sums = jnp.sum(shared(sums, DEPTH_BITS), axis=0)
    both = merge_part(own, rows)
    both, sums = lax.optimization_barrier((both, sums))
    sums = shared(sums, PLANE_BITS).reshape(-1, LANES)
    return combine(both, cols, holo, sums).reshape(2, STRIDE, 1024)


def solution(mesh):
    return jax.shard_map(
        per_device,
        mesh=mesh,
        in_specs=(P(None, "row", "col"), P("row", "col", None)),
        out_specs=P(None, "row", "col"),
        check_vma=False,
    )
```
